512 devices in a mesh: dp: 32 (over z, x), expert: 16 (over y, core).
Axes of the slice: x: 4, y: 8, z: 8, core: 2. Of those that a mesh axis runs over, the one named last changes fastest.
Arguments:
- incoming_vectors: bfloat16 [65536, 1024], P(('dp', 'expert')), may hold values from -6 to 6
- widening_matrix_entries: bfloat16 [704, 32, 1024], P('dp', 'expert'), may hold values from -0.1875 to 0.1875
- switch_input_sums: bfloat16 [704, 327680], P(None, ('dp', 'expert')), may hold values from -8 to 8
- inner_adjoint_signal: bfloat16 [704, 327680], P(None, ('dp', 'expert')), may hold values from -16 to 16
- chosen_specialists: int32 [65536, 6], P(('dp', 'expert')), may hold values from 0 to 31, as said below
- assignment_seat_position: int32 [65536, 6], P(('dp', 'expert')), may hold values from 0 to 127, as said below
- admission_quota: int32 [32], replicated, may hold values from 1 to 20, as said below
Outputs:
- token_grad: bfloat16 [65536, 1024], P(('dp', 'expert'))
- muon_update: float32 [704, 32, 1024], P('dp', 'expert')
The draws below stay inside these ranges and needn't reach their ends.
Inputs may be any that keep to these rules, and one draw needn't show every extreme that they name: `chosen_specialists`: each token names 6 different experts; one expert, which one varies, is named by every token. `assignment_seat_position`: within each aligned block of 128 incoming_vectors (the tokens of one device), the routes to one expert carry the positions 0, 1, ... up to their number minus one, each once. `admission_quota`: the expert named by every token has capacity 20.
All inputs are finite; a program needn't handle non-finite values.
Results may differ from the reference program's by a relative error of at most 0.035.
Values may be sent and summed in bfloat16 or wider, within the bound.
A program may use at most 64 MiB of HBM per device.

```python
import math
import jax
import jax.numpy as jnp
from jax import lax

D = 1024
FF = 704
EXP_DEV = 2
TOP = 6
TOK_DEV = 128
ITERS = 2
EXPERTS = 32
CAP = 20
TOKENS = 65536
ALL_SLOTS = 327680
N_DP = 32
N_EXPERT = 16


def shuffle_one(subkey):
    return jax.random.permutation(subkey, TOK_DEV * TOP)


def routing(key):
    first, second, third, fourth = jax.random.split(key, 4)
    favorite = jax.random.randint(first, (), 0, EXPERTS)
    levels = jax.random.randint(second, (EXPERTS,), 0, 4)
    noise = jax.random.randint(third, (TOKENS, EXPERTS), 0, 1024)
    column = jnp.arange(EXPERTS, dtype=jnp.int32)
    scores = noise + levels * 400 + jnp.where(column == favorite, 1 << 20, 0)
    scores = scores * EXPERTS + column
    ranked_scores, chosen = lax.top_k(scores, TOP)
    blocks = TOKENS // TOK_DEV
    routes = TOK_DEV * TOP
    chosen = chosen.astype(jnp.int32).reshape(blocks, routes)
    shuffle = jax.vmap(shuffle_one)(jax.random.split(fourth, blocks)).astype(jnp.int32)
    composite = chosen * routes + shuffle
    order = jnp.argsort(composite, axis=1)
    sorted_ids = jnp.take_along_axis(chosen, order, axis=1)
    counts = jnp.sum((chosen[..., None] == column).astype(jnp.int32), axis=1)
    starts = jnp.cumsum(counts, axis=1) - counts
    ranked = jnp.arange(routes, dtype=jnp.int32)[None, :] - jnp.take_along_axis(starts, sorted_ids, axis=1)
    inverse = jnp.argsort(order, axis=1)
    positions = jnp.take_along_axis(ranked, inverse, axis=1)
    return (chosen.reshape(TOKENS, TOP), positions.reshape(TOKENS, TOP).astype(jnp.int32), favorite)


def draw_chosen_specialists(key, part):
    shared = routing(key)
    return shared[0]


def draw_assignment_seat_position(key, part):
    shared = routing(key)
    return shared[1]


def draw_admission_quota(key, part):
    shared = routing(key)
    key = jax.random.fold_in(key, 3)
    column = jnp.arange(EXPERTS, dtype=jnp.int32)
    drawn = jax.random.randint(key, (EXPERTS,), max(CAP // 2, 1), CAP + 1)
    return jnp.where(column == shared[2], CAP, drawn).astype(jnp.int32)


def spiked(values, stream_key, source, target, blocks, factor):
    owner, partner = [(jnp.arange(values.shape[position]) // (values.shape[position] // blocks)).reshape([-1 if axis == position else 1 for axis in range(values.ndim)]) for position in (source, target)]
    chosen = jax.random.permutation(stream_key, blocks)[partner]
    strong = (owner == chosen) | (owner == (partner + blocks // 2) % blocks)
    return jnp.where(strong, factor * values, values)


def block_levels(rng, extent, cuts, low, high):
    loudness, own = 1.0, jax.random.fold_in(rng, 6)
    for dim, parts in cuts:
        heights = jnp.exp(jax.random.uniform(jax.random.fold_in(own, dim), (parts,), jnp.float32, low / len(cuts), high / len(cuts)))
        loudness = loudness * jnp.repeat(heights, extent[dim] // parts).reshape([-1 if axis == dim else 1 for axis in range(len(extent))])
    return loudness


def normal_values(stream_key, shape, spread, limit, shards=(), kind=jnp.bfloat16):
    entries = spread * jax.random.normal(stream_key, shape, jnp.float32)
    if shards:
        entries = entries * block_levels(stream_key, shape, shards, -0.22, 0.18)
    return jnp.clip(entries, -limit, limit).astype(kind)


def noise_with(rng, dims, spread, limit, shards, heavy, kind=jnp.bfloat16):
    entries = spread * jax.random.normal(rng, dims, jnp.float32)
    if shards:
        entries = entries * block_levels(rng, dims, shards, -0.22, 0.18)
    return jnp.clip(spiked(entries, jax.random.fold_in(rng, 3), *heavy), -limit, limit).astype(kind)


def setup_inputs(seed: int = 0) -> dict:
    streams_of = jax.random.split(jax.random.key(seed), 8)
    incoming_vectors = normal_values(streams_of[0], (TOKENS, D), 1.0, 6.0, ((0, 512),))
    widening_matrix_entries = normal_values(streams_of[1], (FF, EXPERTS, D), D ** -0.5, 0.1875, ((0, 32), (1, 16)))
    switch_input_sums = normal_values(streams_of[2], (FF, ALL_SLOTS), 1.5, 8.0, ((1, 512),))
    inner_adjoint_signal = noise_with(streams_of[3], (FF, ALL_SLOTS), 1.0, 16.0, ((1, 512),), (1, 0, 64, 4.0))
    chosen_specialists = draw_chosen_specialists(jax.random.fold_in(streams_of[7], 71), 0)
    assignment_seat_position = draw_assignment_seat_position(jax.random.fold_in(streams_of[7], 71), 0)
    admission_quota = draw_admission_quota(jax.random.fold_in(streams_of[7], 71), 0)
    return dict(incoming_vectors=incoming_vectors, widening_matrix_entries=widening_matrix_entries, switch_input_sums=switch_input_sums, inner_adjoint_signal=inner_adjoint_signal, chosen_specialists=chosen_specialists, assignment_seat_position=assignment_seat_position, admission_quota=admission_quota)


quint_a = 3.4445
quint_b = -4.775
quint_c = 2.0315
epsilon = 1e-06

def normalize(grad):
    wide = grad.astype(jnp.float32)
    return (wide / (jnp.sqrt(jnp.sum(wide * wide)) + epsilon)).astype(jnp.bfloat16)

def newton_schulz(iterate):
    for iteration in range(ITERS):
        gram = jnp.dot(iterate, iterate.T, preferred_element_type=jnp.float32).astype(jnp.bfloat16)
        square = jnp.dot(gram, gram, preferred_element_type=jnp.float32)
        poly = (quint_b * gram.astype(jnp.float32) + quint_c * square).astype(jnp.bfloat16)
        iterate = (quint_a * iterate.astype(jnp.float32) + jnp.dot(poly, iterate, preferred_element_type=jnp.float32)).astype(jnp.bfloat16)
    return iterate

def reference(incoming_vectors, widening_matrix_entries, switch_input_sums, inner_adjoint_signal, chosen_specialists, assignment_seat_position, admission_quota):
    blocks = N_DP * N_EXPERT
    slot_total = EXPERTS * CAP
    surviving_flags = assignment_seat_position < admission_quota[chosen_specialists]
    targets = jnp.where(surviving_flags, chosen_specialists * CAP + assignment_seat_position, slot_total).astype(jnp.int32)
    targets = targets.reshape(blocks, TOK_DEV * TOP)
    token_rows = incoming_vectors.reshape(blocks, TOK_DEV, D)

    def fill_block(inputs):
        block_targets, block_tokens = inputs
        values = jnp.repeat(block_tokens, TOP, axis=0)
        buffer = jnp.zeros((slot_total + 1, D), incoming_vectors.dtype).at[block_targets].set(values)
        return buffer[:slot_total]
    sends = lax.map(fill_block, (targets, token_rows))
    sends = sends.reshape(N_DP, N_EXPERT, N_EXPERT, EXP_DEV, CAP, D)
    gate_grid = switch_input_sums.reshape(FF, N_DP, N_EXPERT, N_EXPERT, EXP_DEV, CAP)
    hidden_grid = inner_adjoint_signal.reshape(FF, N_DP, N_EXPERT, N_EXPERT, EXP_DEV, CAP)
    scale = 0.2 * math.sqrt(max(FF, D))

    def one_expert(expert):
        owner = expert // EXP_DEV
        slot_local = expert % EXP_DEV
        gate_part = lax.dynamic_index_in_dim(lax.dynamic_index_in_dim(gate_grid, owner, 2, keepdims=False), slot_local, 3, keepdims=False)
        hidden_part = lax.dynamic_index_in_dim(lax.dynamic_index_in_dim(hidden_grid, owner, 2, keepdims=False), slot_local, 3, keepdims=False)
        up_grad = (hidden_part.astype(jnp.float32) * jax.nn.silu(gate_part.astype(jnp.float32))).astype(jnp.bfloat16)
        inputs = lax.dynamic_index_in_dim(lax.dynamic_index_in_dim(sends, owner, 2, keepdims=False), slot_local, 2, keepdims=False)
        partial_value = jnp.einsum('fdjp,djpc->dfc', up_grad.astype(jnp.float32), inputs.astype(jnp.float32)).astype(jnp.bfloat16)
        grad = lax.optimization_barrier(jnp.sum(partial_value.astype(jnp.float32), axis=0)).astype(jnp.bfloat16)
        update = scale * newton_schulz(normalize(grad)).astype(jnp.float32)
        weight = lax.dynamic_index_in_dim(widening_matrix_entries, expert, 1, keepdims=False)
        slot_grad = jnp.einsum('fdjp,fc->djpc', up_grad.astype(jnp.float32), weight.astype(jnp.float32)).astype(jnp.bfloat16)
        return (update, slot_grad)
    updates, slot_grads = lax.map(one_expert, jnp.arange(EXPERTS, dtype=jnp.int32))
    ids_grid = chosen_specialists.reshape(N_DP, N_EXPERT, TOK_DEV, TOP)
    pos_grid = assignment_seat_position.reshape(N_DP, N_EXPERT, TOK_DEV, TOP)
    keep_grid = surviving_flags.reshape(N_DP, N_EXPERT, TOK_DEV, TOP)

    def row_grads(inputs):
        row_index, ids_row, pos_row, keep_row = inputs
        grads_row = lax.dynamic_index_in_dim(slot_grads, row_index, 1, keepdims=False)
        source = jnp.arange(N_EXPERT, dtype=jnp.int32)[:, None, None]
        picked = grads_row[ids_row, source, jnp.where(keep_row, pos_row, 0).astype(jnp.int32)]
        summed = lax.optimization_barrier(jnp.sum(jnp.where(keep_row[..., None], picked.astype(jnp.float32), jnp.float32(0.0)), axis=2))
        return summed.astype(jnp.bfloat16)
    token_grad = lax.map(row_grads, (jnp.arange(N_DP, dtype=jnp.int32), ids_grid, pos_grid, keep_grid))
    token_grad = token_grad.reshape(TOKENS, D)
    return (token_grad, jnp.transpose(updates, (1, 0, 2)))
```

```python
import math

import jax
import jax.numpy as jnp
import numpy as np
from jax import lax
from jax.experimental import pallas as pl
from jax.experimental.pallas import tpu as pltpu
from jax.sharding import PartitionSpec as P

MESH = pl.DeviceIdType.MESH
F32 = jnp.float32
BF16 = jnp.bfloat16

ITERS = 2
QUINT_A = 3.4445
QUINT_B = -4.775
QUINT_C = 2.0315
EPSILON = 1e-06

NX, NY, NZ = 4, 8, 8
NE = 2 * NY
FF, D = 704, 1024
TOK, TOP = 128, 6
CAP = 20
SLOTS = 2 * NE * CAP
ROWS = FF // (NX * NZ)
WBLK = 48
SEAT = 24
EM = 2 * NE * SEAT
HALF = FF // 2
PIECE = TOK // 2

UP, DOWN = 0, 1


def layout_tables():
    table = np.full((8, NX * NZ * WBLK), -1, np.int32)
    for j in range(NE):
        for l in range(2):
            for p in range(CAP):
                s = (j * 2 + l) * CAP + p
                table[0, l * (EM // 2) + j * SEAT + p] = s
                table[1, s] = j * WBLK + l * SEAT + p
    for d in range(NX * NZ):
        for l in range(2):
            for i in range(ROWS):
                table[2, d * WBLK + l * ROWS + i] = d * ROWS + i
                table[3, d * WBLK + l * ROWS + i] = l
    return table


def dot(a, b):
    return jnp.dot(a, b, preferred_element_type=F32)


def dot_nt(a, b):
    return lax.dot_general(a, b, (((1,), (1,)), ((), ())), preferred_element_type=F32)


def kernel(
    tok_ref,
    w_ref,
    gate_ref,
    adj_ref,
    chosen_ref,
    seat_ref,
    quota_ref,
    lay_ref,
    out_tok,
    out_mu,
    tokv,
    wst,
    tbl,
    u_ref,
    uem,
    utj,
    ustt,
    slots,
    part,
    fromopp,
    rsum,
    xrecv,
    zsend,
    zown,
    zrecv,
    sg,
    ret,
    grad,
    x0_ref,
    x1_ref,
    gram,
    poly,
    rows_ref,
    fin,
    t_s,
    t_r,
    y_s,
    y_r,
    c_s,
    c_r,
    z_s,
    z_r,
    wx_s,
    wx_r,
    wf_s,
    wf_r,
    opp_s,
    opp_r,
    rel_s,
    rel_r,
    zp_s,
    zp_r,
    ag_s,
    ag_r,
    rt_s,
    rt_r,
    fn_s,
    fn_r,
):
    dp = lax.axis_index("dp")
    me = lax.axis_index("expert")
    x, z = lax.rem(dp, NX), dp // NX
    y, c = me // 2, lax.rem(me, 2)

    def wrap(v, n):
        return lax.rem(v + 2 * n, n)

    def peer(dx=0, dy=0, dz=0, dc=0):
        core = lax.rem(c + dc, 2)
        return (wrap(z + dz, NZ) * NX + wrap(x + dx, NX), wrap(y + dy, NY) * 2 + core)

    def copy(ref_src, ref_dst, ssem, rsem, device):
        return pltpu.make_async_remote_copy(
            src_ref=ref_src,
            dst_ref=ref_dst,
            send_sem=ssem,
            recv_sem=rsem,
            device_id=device,
            device_id_type=MESH,
        )

    def aligned(v, m):
        return pl.multiple_of(v, m)

    barrier = pltpu.get_barrier_semaphore()
    greeted = [(dp, lax.rem(me + i, NE)) for i in range(1, NE)]
    greeted += [peer(dz=k) for k in range(1, NZ)]
    greeted += [peer(dx=k) for k in range(1, NX)]
    for device in greeted:
        pl.semaphore_signal(barrier, inc=1, device_id=device, device_id_type=MESH)

    chosen = chosen_ref[...]
    quota = jnp.zeros_like(chosen)
    for e in range(2 * NE):
        quota = jnp.where(chosen == e, quota_ref[e], quota)
    code = jnp.where(seat_ref[...] < quota, chosen * 32 + seat_ref[...], -1)
    tbl[me, 0:TOP, :] = code
    tbl[me, TOP:8, :] = jnp.full((8 - TOP, TOK), -1, jnp.int32)

    def tok_rows(yb, cb, p):
        return pl.ds(aligned(yb * (2 * TOK) + cb * TOK + p * PIECE, PIECE), PIECE)

    own_rows = pl.ds(aligned(y * (2 * TOK) + c * TOK, TOK), TOK)
    tokv[own_rows, :] = tok_ref[...]

    def w_rows(zb, xb):
        return pl.ds(aligned((zb * NX + xb) * WBLK, WBLK), WBLK)

    wst[w_rows(z, x), :] = w_ref[...]

    pl.semaphore_wait(barrier, len(greeted))

    sent = []

    def start(cp):
        cp.start()
        sent.append(cp)

    rel = [0, -1, 1, -2, 2, -3, 3, 4]

    def y_copy(direction, hop, p):
        step = 1 if direction == UP else -1
        yb = wrap(y - step * (hop - 1), NY)
        view = tokv.at[tok_rows(yb, c, p), :]
        at = (direction, hop - 1, p)
        return copy(view, view, y_s.at[at], y_r.at[at], peer(dy=step))

    def y_arrival(direction, hop, p):
        step = 1 if direction == UP else -1
        yb = wrap(y - step * hop, NY)
        view = tokv.at[tok_rows(yb, c, p), :]
        at = (direction, hop - 1, p)
        return yb, copy(view, view, y_s.at[at], y_r.at[at], peer(dy=step))

    def to_sibling(n, p):
        yb = wrap(y + rel[n], NY)
        view = tokv.at[tok_rows(yb, c, p), :]
        start(copy(view, view, c_s.at[n, p], c_r.at[n, p], peer(dc=1)))

    def y_recv(direction, hop, p):
        _, cp = y_arrival(direction, hop, p)
        cp.wait_recv()
        if hop < 3 or (hop == 3 and p == direction):
            start(y_copy(direction, hop + 1, p))
        step = 1 if direction == UP else -1
        n = rel.index(-step * hop) if hop < 4 else 7
        to_sibling(n, p)

    left, right = slice(0, D // 2), slice(D // 2, D)

    def z_view(zb, xb, hop, direction):
        if hop < 4:
            return wst.at[w_rows(zb, xb), :]
        return wst.at[w_rows(zb, xb), left if direction == UP else right]

    def z_copy(direction, hop):
        step = 1 if direction == UP else -1
        zb = wrap(z - step * (hop - 1), NZ)
        view = z_view(zb, x, hop, direction)
        at = (direction, hop - 1)
        return copy(view, view, z_s.at[at], z_r.at[at], peer(dz=step))

    def x_sends(n):
        zb = wrap(z + rel[n], NZ)
        view = wst.at[w_rows(zb, x), :]
        for direction, step in ((UP, 1), (DOWN, -1)):
            at = (direction, n)
            start(copy(view, view, wx_s.at[at], wx_r.at[at], peer(dx=step)))

    def z_recv(hop):
        for direction, step in ((UP, 1), (DOWN, -1)):
            zb = wrap(z - step * hop, NZ)
            view = z_view(zb, x, hop, direction)
            at = (direction, hop - 1)
            copy(view, view, z_s.at[at], z_r.at[at], peer(dz=step)).wait_recv()
            if hop < 4:
                start(z_copy(direction, hop + 1))
                x_sends(rel.index(-step * hop))
        if hop == 4:
            x_sends(7)

    def x_recv(n):
        zb = wrap(z + rel[n], NZ)
        for direction, step in ((UP, 1), (DOWN, -1)):
            rows = w_rows(zb, wrap(x - step, NX))
            at = (direction, n)
            view = wst.at[rows, :]
            copy(view, view, wx_s.at[at], wx_r.at[at], peer(dx=step)).wait_recv()
            view = wst.at[rows, left if direction == UP else right]
            start(copy(view, view, wf_s.at[at], wf_r.at[at], peer(dx=step)))

    def xf_wait(n):
        zb = wrap(z + rel[n], NZ)
        rows = w_rows(zb, wrap(x + 2, NX))
        for direction, step in ((UP, 1), (DOWN, -1)):
            at = (direction, n)
            view = wst.at[rows, left if direction == UP else right]
            copy(view, view, wf_s.at[at], wf_r.at[at], peer(dx=step)).wait_recv()

    def up_grad():
        def tile(t, carry):
            rows = pl.ds(aligned(t * 64, 64), 64)
            g = gate_ref[rows, :].astype(F32)
            a = adj_ref[rows, :].astype(F32)
            u_ref[rows, :] = (a * (g / (1.0 + jnp.exp(-g)))).astype(BF16)
            return carry

        lax.fori_loop(0, FF // 64, tile, 0)

    def expert_major():
        pick = jnp.where(
            lax.broadcasted_iota(jnp.int32, (SLOTS, EM), 0) == lay_ref[0:1, 0:EM], 1.0, 0.0
        ).astype(BF16)
        for t in range(2):
            rows = slice(t * HALF, (t + 1) * HALF)
            uem[rows, :] = dot(u_ref[rows, :], pick).astype(BF16)

    def source_major():
        pick = jnp.where(
            lax.broadcasted_iota(jnp.int32, (EM, SLOTS), 0) == lay_ref[1:2, 0:SLOTS], 1.0, 0.0
        ).astype(BF16)
        utj[...] = dot_nt(pick, u_ref[...]).astype(BF16)

    def stacked(t):
        cols = slice(t * 512, (t + 1) * 512)
        pick = jnp.where(
            lax.broadcasted_iota(jnp.int32, (FF, 512), 0) == lay_ref[2:3, cols], 1.0, 0.0
        ).astype(BF16)
        which = lay_ref[3:4, cols]
        local = lax.broadcasted_iota(jnp.int32, (2 * WBLK, 512), 0)
        row_expert = jnp.where(
            local < WBLK, jnp.where(local < SEAT, 0, 1), jnp.where(local < WBLK + SEAT, 0, 1)
        )
        keep = row_expert == which
        full = dot(utj[...], pick)
        for s in range(EM // (2 * WBLK)):
            rows = slice(s * 2 * WBLK, (s + 1) * 2 * WBLK)
            ustt[rows, cols] = jnp.where(keep, full[rows, :], 0.0).astype(BF16)

    def one_hot(yb, cb, l):
        want = lax.broadcasted_iota(jnp.int32, (SEAT, TOK), 0) + (2 * me + l) * 32
        codes = tbl[yb * 2 + cb]
        hit = jnp.zeros((SEAT, TOK), F32)
        for k in range(TOP):
            hit = hit + jnp.where(codes[k : k + 1, :] == want, 1.0, 0.0)
        return hit

    def gather(n):
        yb = wrap(y + rel[n], NY)
        for p in range(2):
            view = tokv.at[tok_rows(yb, 1 - c, p), :]
            copy(view, view, c_s.at[n, p], c_r.at[n, p], peer(dc=1)).wait_recv()
        zero = jnp.zeros((SEAT, TOK), F32)
        blocks = []
        for l in range(2):
            blocks.append(jnp.concatenate([one_hot(yb, 0, l), zero], axis=1))
            blocks.append(jnp.concatenate([zero, one_hot(yb, 1, l)], axis=1))
        pick = jnp.concatenate(blocks, axis=0).astype(BF16)
        tokens = tokv[pl.ds(aligned(yb * 2 * TOK, 2 * TOK), 2 * TOK), :]
        got = dot(pick, tokens).astype(BF16)
        rows = pl.ds(aligned(yb * 2 * SEAT, 2 * SEAT), 2 * SEAT)
        slots[0, rows, :] = got[0 : 2 * SEAT, :]
        slots[1, rows, :] = got[2 * SEAT :, :]

    for i in range(1, NE):
        j = lax.rem(me + i, NE)
        start(copy(tbl.at[me], tbl.at[me], t_s.at[i], t_r.at[i], (dp, j)))
    for p in range(2):
        for direction in (UP, DOWN):
            start(y_copy(direction, 1, p))
    for direction in (UP, DOWN):
        start(z_copy(direction, 1))
    x_sends(0)
    for p in range(2):
        to_sibling(0, p)

    def y_both(hop, p):
        y_recv(UP, hop, p)
        y_recv(DOWN, hop, p)

    up_grad()
    y_both(1, 0)
    z_recv(1)
    x_recv(0)
    expert_major()
    y_both(1, 1)
    x_recv(1)
    source_major()
    y_both(2, 0)
    z_recv(2)
    x_recv(2)
    stacked(0)
    y_both(2, 1)
    x_recv(3)
    for i in range(1, NE):
        j = lax.rem(me + NE - i, NE)
        copy(tbl.at[j], tbl.at[j], t_s.at[i], t_r.at[i], (dp, j)).wait_recv()
    gather(0)
    gather(1)
    y_both(3, 0)
    z_recv(3)
    gather(2)
    stacked(1)
    x_recv(4)
    y_both(3, 1)
    z_recv(4)
    stacked(2)
    gather(3)
    x_recv(5)
    gather(4)
    y_recv(UP, 4, 0)
    y_recv(DOWN, 4, 1)
    gather(5)
    gather(6)
    gather(7)

    r0 = wrap(x - 2 * c, NX)
    is_owner = r0 < 2
    l_other = lax.rem(r0, 2)
    l_relay = 1 - l_other
    is_plus = jnp.logical_or(r0 == 1, r0 == 2)
    b_relay = jnp.where(is_plus, 0, 1)
    h_direct = jnp.where(is_plus, HALF, 0)
    h_sum = HALF - h_direct
    toward = jnp.where(is_plus, -1, 1)
    owner_dev = peer(dx=toward)
    opp_dev = peer(dx=-toward)
    z2 = z // 2
    order = [wrap(z2 + k, 4) for k in (2, 1, 3, 0)]

    def cols2(i):
        return pl.ds(aligned(order[i] * 256, 256), 256)

    def halfrows(h):
        return pl.ds(aligned(h, HALF), HALF)

    def direct_copy(i):
        return copy(
            part.at[l_relay, halfrows(h_direct), cols2(i)],
            xrecv.at[b_relay, halfrows(h_direct), cols2(i)],
            rel_s.at[0, i],
            rel_r.at[b_relay, 0, i],
            owner_dev,
        )

    def summed_copy(i):
        return copy(
            rsum.at[:, cols2(i)],
            xrecv.at[b_relay, halfrows(h_sum), cols2(i)],
            rel_s.at[1, i],
            rel_r.at[b_relay, 1, i],
            owner_dev,
        )

    def opp_copy(i, h):
        return copy(
            part.at[l_other, pl.ds(h * HALF, HALF), cols2(i)],
            fromopp.at[:, cols2(i)],
            opp_s.at[h, i],
            opp_r.at[i],
            peer(dx=-1 if h == 0 else 1),
        )

    def partials(i):
        for l in range(2):
            right_side = slots[l, :, cols2(i)]
            for t in range(2):
                rows = slice(t * HALF, (t + 1) * HALF)
                part[l, rows, cols2(i)] = dot(
                    uem[rows, l * (EM // 2) : (l + 1) * (EM // 2)], right_side
                ).astype(BF16)
        start(direct_copy(i))

        @pl.when(jnp.logical_not(is_owner))
        def _():
            opp_copy(i, 0).start()
            opp_copy(i, 1).start()

    def relay(i):
        opp = fromopp.at[:, cols2(i)]
        copy(opp, opp, opp_s.at[0, i], opp_r.at[i], opp_dev).wait_recv()
        rsum[:, cols2(i)] = (
            part[l_relay, halfrows(h_sum), cols2(i)].astype(F32) + fromopp[:, cols2(i)].astype(F32)
        ).astype(BF16)
        start(summed_copy(i))

    def z_part(i, k):
        zeta = order[i] * 2 + k
        view = zsend.at[:, pl.ds(aligned(zeta * 128, 128), 128)]
        return copy(view, zrecv.at[z], zp_s.at[i, k], zp_r.at[z], (zeta * NX + x, me))

    def finish(i):
        @pl.when(is_owner)
        def _():
            for b in range(2):
                for kind in range(2):
                    h = (1 - b) * HALF if kind == 0 else b * HALF
                    view = xrecv.at[b, pl.ds(h, HALF), cols2(i)]
                    copy(
                        view, view, rel_s.at[0, i], rel_r.at[b, kind, i], peer(dx=1 if b == 0 else -1)
                    ).wait_recv()
            total = (
                part[l_other, :, cols2(i)].astype(F32)
                + xrecv[0, :, cols2(i)].astype(F32)
                + xrecv[1, :, cols2(i)].astype(F32)
            )
            zsend[:, cols2(i)] = total.astype(BF16)
            if i < 3:
                z_part(i, 0).start()
                z_part(i, 1).start()
            else:

                @pl.when(lax.rem(z, 2) == 0)
                def _():
                    z_part(i, 1).start()
                    zown[...] = total[:, 0:128]

                @pl.when(lax.rem(z, 2) == 1)
                def _():
                    z_part(i, 0).start()
                    zown[...] = total[:, 128:256]

    def slot_grads(n):
        cols = slice(n * 256, (n + 1) * 256)
        sg[:, cols] = dot(ustt[...], wst[:, cols]).astype(BF16)

    def block_rows(j):
        return pl.ds(aligned(j * WBLK, WBLK), WBLK)

    partials(0)
    partials(1)
    x_recv(6)
    x_recv(7)
    relay(0)
    partials(2)
    relay(1)
    partials(3)
    for n in range(8):
        xf_wait(n)
    slot_grads(0)
    finish(0)
    slot_grads(1)
    relay(2)
    slot_grads(2)
    finish(1)
    slot_grads(3)
    for i in range(1, NE):
        j = lax.rem(me + i, NE)
        start(
            copy(
                sg.at[block_rows(j), :],
                ret.at[block_rows(me), :],
                rt_s.at[i],
                rt_r.at[i],
                (dp, j),
            )
        )
    ret[block_rows(me), :] = sg[block_rows(me), :]
    relay(3)
    finish(2)
    finish(3)

    zcols = pl.ds(aligned(z * 128, 128), 128)

    def ag_view(zb, p):
        return grad.at[pl.ds(p * HALF, HALF), pl.ds(aligned(zb * 128, 128), 128)]

    def ag_copy(direction, hop, p):
        step = 1 if direction == UP else -1
        view = ag_view(wrap(z - step * (hop - 1), NZ), p)
        at = (direction, hop - 1, p)
        return copy(view, view, ag_s.at[at], ag_r.at[at], peer(dz=step))

    def ag_recv(direction, hop, p):
        step = 1 if direction == UP else -1
        view = ag_view(wrap(z - step * hop, NZ), p)
        at = (direction, hop - 1, p)
        copy(view, view, ag_s.at[at], ag_r.at[at], peer(dz=step)).wait_recv()
        if hop < 3 or (hop == 3 and p == direction):
            ag_copy(direction, hop + 1, p).start()

    def rows_copy(k):
        xd = wrap(x + k, NX)
        return copy(
            rows_ref.at[pl.ds(aligned(xd * 32, 32), 32), :],
            fin.at[l_other],
            fn_s.at[k],
            fn_r.at[l_other],
            peer(dx=k),
        )

    @pl.when(is_owner)
    def _():
        total = zown[...]
        for k in range(1, NZ):
            src = wrap(z + k, NZ)
            view = zrecv.at[src]
            copy(view, view, zp_s.at[0, 0], zp_r.at[src], peer(dz=k)).wait_recv()
            total = total + zrecv[src].astype(F32)
        grad[:, zcols] = total.astype(BF16)
        for p in range(2):
            for direction in (UP, DOWN):
                ag_copy(direction, 1, p).start()
        for hop in range(1, 4):
            for p in range(2):
                for direction in (UP, DOWN):
                    ag_recv(direction, hop, p)
        ag_recv(UP, 4, 0)
        ag_recv(DOWN, 4, 1)

        wide = grad[...].astype(F32)
        squares = jnp.sum(jnp.sum(wide * wide, axis=0, keepdims=True), axis=1, keepdims=True)
        inverse = 1.0 / (jnp.sqrt(squares) + EPSILON)
        x0_ref[...] = (wide * inverse).astype(BF16)

        halves = [slice(0, HALF), slice(HALF, FF)]

        def grams(it):
            for rows in halves:
                gram[rows, :] = dot_nt(it[rows, :], it[...]).astype(BF16)

        grams(x0_ref)
        for rows in halves:
            square = dot(gram[rows, :], gram[...])
            poly[rows, :] = (QUINT_B * gram[rows, :].astype(F32) + QUINT_C * square).astype(BF16)
        for rows in halves:
            x1_ref[rows, :] = (
                QUINT_A * x0_ref[rows, :].astype(F32) + dot(poly[rows, :], x0_ref[...])
            ).astype(BF16)
        grams(x1_ref)
        picks = []
        for xd in range(NX):
            r = lax.broadcasted_iota(jnp.int32, (32, FF), 0)
            f = lax.broadcasted_iota(jnp.int32, (32, FF), 1)
            hit = jnp.logical_and(r < ROWS, f == r + (z * NX + xd) * ROWS)
            picks.append(jnp.where(hit, 1.0, 0.0))
        pick = jnp.concatenate(picks, axis=0).astype(BF16)
        gram_rows = dot(pick, gram[...]).astype(BF16)
        it_rows = dot(pick, x1_ref[...])
        poly_rows = (QUINT_B * gram_rows.astype(F32) + QUINT_C * dot(gram_rows, gram[...])).astype(
            BF16
        )
        rows_ref[...] = (QUINT_A * it_rows + dot(poly_rows, x1_ref[...])).astype(BF16)
        for k in range(1, NX):
            rows_copy(k).start()
        fin[l_other] = rows_ref[pl.ds(aligned(x * 32, 32), 32), :]

    for i in range(1, NE):
        j = lax.rem(me + NE - i, NE)
        view = ret.at[block_rows(j), :]
        copy(view, view, rt_s.at[i], rt_r.at[i], (dp, j)).wait_recv()
    hits = []
    for e in range(2 * NE):
        want = lax.broadcasted_iota(jnp.int32, (SEAT, TOK), 0) + e * 32
        hit = jnp.zeros((SEAT, TOK), F32)
        for k in range(TOP):
            hit = hit + jnp.where(code[k : k + 1, :] == want, 1.0, 0.0)
        hits.append(hit)
    pick = jnp.concatenate(hits, axis=0).T.astype(BF16)
    out_tok[...] = dot(pick, ret[...]).astype(BF16)

    scale = 0.2 * math.sqrt(max(FF, D))
    for l in range(2):
        owner_x = 2 * c + l

        @pl.when(x != owner_x)
        def _():
            view = fin.at[l]
            copy(view, view, fn_s.at[1], fn_r.at[l], peer(dx=1)).wait_recv()

        out_mu[:, l, :] = scale * fin[l, 0:ROWS, :].astype(F32)

    for cp in sent:
        cp.wait_send()

    @pl.when(jnp.logical_not(is_owner))
    def _():
        for i in range(4):
            opp_copy(i, 0).wait_send()
            opp_copy(i, 1).wait_send()

    @pl.when(is_owner)
    def _():
        for i in range(3):
            z_part(i, 0).wait_send()
            z_part(i, 1).wait_send()

        @pl.when(lax.rem(z, 2) == 0)
        def _():
            z_part(3, 1).wait_send()

        @pl.when(lax.rem(z, 2) == 1)
        def _():
            z_part(3, 0).wait_send()

        for hop in range(1, 5):
            for p in range(2):
                for direction in (UP, DOWN):
                    if hop < 4 or p == direction:
                        ag_copy(direction, hop, p).wait_send()
        for k in range(1, NX):
            rows_copy(k).wait_send()


def body(tokens, weights, gate, adjoint, chosen, seat, quota):
    stacked_w = jnp.concatenate(
        [weights[:, 0, :], weights[:, 1, :], jnp.zeros((WBLK - 2 * ROWS, D), BF16)], axis=0
    )
    vmem = pl.BlockSpec(memory_space=pltpu.VMEM)
    sem = pltpu.SemaphoreType.DMA
    scratch = [
        pltpu.VMEM((NE * TOK, D), BF16),
        pltpu.VMEM((NX * NZ * WBLK, D), BF16),
        pltpu.VMEM((NE, 8, TOK), jnp.int32),
        pltpu.VMEM((FF, SLOTS), BF16),
        pltpu.VMEM((FF, EM), BF16),
        pltpu.VMEM((EM, FF), BF16),
        pltpu.VMEM((EM, NX * NZ * WBLK), BF16),
        pltpu.VMEM((2, EM // 2, D), BF16),
        pltpu.VMEM((2, FF, D), BF16),
        pltpu.VMEM((HALF, D), BF16),
        pltpu.VMEM((HALF, D), BF16),
        pltpu.VMEM((2, FF, D), BF16),
        pltpu.VMEM((FF, D), BF16),
        pltpu.VMEM((FF, 128), F32),
        pltpu.VMEM((NZ, FF, 128), BF16),
        pltpu.VMEM((EM, D), BF16),
        pltpu.VMEM((EM, D), BF16),
        pltpu.VMEM((FF, D), BF16),
        pltpu.VMEM((FF, D), BF16),
        pltpu.VMEM((FF, D), BF16),
        pltpu.VMEM((FF, FF), BF16),
        pltpu.VMEM((FF, FF), BF16),
        pltpu.VMEM((128, D), BF16),
        pltpu.VMEM((2, 32, D), BF16),
        sem((NE,)),
        sem((NE,)),
        sem((2, 4, 2)),
        sem((2, 4, 2)),
        sem((8, 2)),
        sem((8, 2)),
        sem((2, 4)),
        sem((2, 4)),
        sem((2, 8)),
        sem((2, 8)),
        sem((2, 8)),
        sem((2, 8)),
        sem((2, 4)),
        sem((4,)),
        sem((2, 4)),
        sem((2, 2, 4)),
        sem((4, 2)),
        sem((NZ,)),
        sem((2, 4, 2)),
        sem((2, 4, 2)),
        sem((NE,)),
        sem((NE,)),
        sem((NX,)),
        sem((2,)),
    ]
    return pl.pallas_call(
        kernel,
        out_shape=(
            jax.ShapeDtypeStruct((TOK, D), BF16),
            jax.ShapeDtypeStruct((ROWS, 2, D), F32),
        ),
        in_specs=[vmem] * 6 + [pl.BlockSpec(memory_space=pltpu.SMEM), vmem],
        out_specs=(vmem, vmem),
        scratch_shapes=scratch,
        compiler_params=pltpu.CompilerParams(
            collective_id=0, has_side_effects=True, vmem_limit_bytes=60 * 2**20
        ),
        cost_estimate=pl.CostEstimate(
            flops=16 * 10**9, bytes_accessed=5 * 10**6, transcendentals=450560
        ),
        name="expert_backward",
    )(tokens, stacked_w, gate, adjoint, chosen.T, seat.T, quota, jnp.asarray(layout_tables()))


def solution(mesh):
    return jax.shard_map(
        body,
        mesh=mesh,
        in_specs=(
            P(("dp", "expert"), None),
            P("dp", "expert", None),
            P(None, ("dp", "expert")),
            P(None, ("dp", "expert")),
            P(("dp", "expert"), None),
            P(("dp", "expert"), None),
            P(),
        ),
        out_specs=(P(("dp", "expert"), None), P("dp", "expert", None)),
        check_vma=False,
    )
```

```python
import math

import jax
import jax.numpy as jnp
import numpy as np
from jax import lax
from jax.experimental import pallas as pl
from jax.experimental.pallas import tpu as pltpu
from jax.sharding import PartitionSpec as P

MESH = pl.DeviceIdType.MESH
F32 = jnp.float32
BF16 = jnp.bfloat16

ITERS = 2
QUINT_A = 3.4445
QUINT_B = -4.775
QUINT_C = 2.0315
EPSILON = 1e-06

NX, NY, NZ = 4, 8, 8
NE = 2 * NY
FF, D = 704, 1024
TOK, TOP = 128, 6
CAP = 20
SLOTS = 2 * NE * CAP
ROWS = FF // (NX * NZ)
WBLK = 48
GROUP = 4 * CAP
SLOTS_E = NE * CAP
DEPTH = 384
WROWS = 2 * ROWS
ZBLK = NX * WROWS
WALL = NZ * ZBLK
ZPIECES = ((0, 96), (96, ZBLK - 96))
REL = (0, -1, 1, -2, 2, -3, 3, 4)
HALF = FF // 2
PIECE = TOK // 2

UP, DOWN = 0, 1


def layout_tables():
    table = np.full((8, WALL), -1, np.int32)
    table[1, :] = -(1 << 20)
    for n in range(NY):
        for core in range(2):
            for p in range(CAP):
                at = (n * 2 + core) * CAP + p
                table[0, at] = REL[n] % NY
                table[1, at] = core * 2 * CAP + p
    for j in range(NE):
        for l in range(2):
            for p in range(CAP):
                table[2, (j * 2 + l) * CAP + p] = l
    for d in range(NX * NZ):
        for l in range(2):
            for i in range(ROWS):
                table[3, d * WROWS + l * ROWS + i] = d * ROWS + i
                table[4, d * WROWS + l * ROWS + i] = l
    for k in range(NX):
        for i in range(WROWS):
            table[5, k * WBLK + i] = k * WROWS + i
    return table


def dot(a, b):
    return jnp.dot(a, b, preferred_element_type=F32)


def dot_nt(a, b):
    return lax.dot_general(a, b, (((1,), (1,)), ((), ())), preferred_element_type=F32)


def kernel(
    tok_hbm,
    w_hbm,
    gate_hbm,
    adj_hbm,
    chosen_hbm,
    seat_hbm,
    quota_ref,
    lay_hbm,
    out_tok,
    out_mu,
    w_ref,
    gate_ref,
    adj_ref,
    chosen_ref,
    seat_ref,
    lay_ref,
    in_s,
    tokv,
    wx,
    wst,
    tbl,
    u_ref,
    uown,
    utail,
    utails,
    ucat,
    utj,
    ustt,
    sown,
    scat,
    zsend,
    zown,
    zrecv,
    sg,
    ret,
    grad,
    x1_ref,
    gram_sum,
    gram,
    poly,
    rows_ref,
    fin,
    t_s,
    t_r,
    y_s,
    y_r,
    c_s,
    c_r,
    w_s,
    w_r,
    z_s,
    z_r,
    uc_s,
    uc_r,
    sc_s,
    sc_r,
    zp_s,
    zp_r,
    ag_s,
    ag_r,
    rt_s,
    rt_r,
    fn_s,
    fn_r,
    picked,
    for_sibling,
    from_sibling,
    sib_s,
    sib_r,
):
    dp = lax.axis_index("dp")
    me = lax.axis_index("expert")
    x, z = lax.rem(dp, NX), dp // NX
    y, c = me // 2, lax.rem(me, 2)

    def wrap(v, n):
        return lax.rem(v + 2 * n, n)

    def peer(dx=0, dy=0, dz=0, dc=0):
        core = lax.rem(c + dc, 2)
        return (wrap(z + dz, NZ) * NX + wrap(x + dx, NX), wrap(y + dy, NY) * 2 + core)

    def copy(ref_src, ref_dst, ssem, rsem, device):
        return pltpu.make_async_remote_copy(
            src_ref=ref_src,
            dst_ref=ref_dst,
            send_sem=ssem,
            recv_sem=rsem,
            device_id=device,
            device_id_type=MESH,
        )

    def aligned(v, m):
        return pl.multiple_of(v, m)

    barrier = pltpu.get_barrier_semaphore()
    greeted = [(dp, lax.rem(me + i, NE)) for i in range(1, NE)]
    greeted += [peer(dz=k) for k in range(1, NZ)]
    greeted += [peer(dx=k) for k in range(1, NX)]
    for device in greeted:
        pl.semaphore_signal(barrier, inc=1, device_id=device, device_id_type=MESH)

    own_rows = pl.ds(aligned(y * (2 * TOK) + c * TOK, TOK), TOK)
    operands = (
        (tok_hbm, tokv.at[own_rows, :]),
        (w_hbm, w_ref),
        (chosen_hbm, chosen_ref),
        (seat_hbm, seat_ref),
        (lay_hbm, lay_ref),
        (gate_hbm, gate_ref),
        (adj_hbm, adj_ref),
    )
    loads = [pltpu.make_async_copy(a, b, in_s.at[i]) for i, (a, b) in enumerate(operands)]
    for cp in loads:
        cp.start()
    for cp in loads[:4]:
        cp.wait()

    chosen = chosen_ref[...]
    quota = jnp.zeros_like(chosen)
    for e in range(2 * NE):
        quota = jnp.where(chosen == e, quota_ref[e], quota)
    code = jnp.where(seat_ref[...] < quota, chosen * 32 + seat_ref[...], -1)
    tbl[me, 0:TOP, :] = code
    tbl[me, TOP:8, :] = jnp.full((8 - TOP, TOK), -1, jnp.int32)

    def tok_rows(yb, cb, p):
        return pl.ds(aligned(yb * (2 * TOK) + cb * TOK + p * PIECE, PIECE), PIECE)

    def wx_rows(xb):
        return pl.ds(aligned(xb * WBLK, WBLK), WBLK)

    blank = jnp.zeros((WBLK - 2 * ROWS, D), BF16)
    wx[wx_rows(x), :] = jnp.concatenate([w_ref[:, 0, :], w_ref[:, 1, :], blank], axis=0)
    for k in range(NX):
        scat[k * DEPTH + SLOTS_E : (k + 1) * DEPTH, :] = jnp.zeros((DEPTH - SLOTS_E, D), BF16)

    r0 = wrap(x - 2 * c, NX)
    is_owner = r0 < 2
    l_own = lax.rem(r0, 2)

    pl.semaphore_wait(barrier, len(greeted))

    sent = []

    def start(cp):
        cp.start()
        sent.append(cp)

    def y_copy(direction, hop, p):
        step = 1 if direction == UP else -1
        yb = wrap(y - step * (hop - 1), NY)
        view = tokv.at[tok_rows(yb, c, p), :]
        at = (direction, hop - 1, p)
        return copy(view, view, y_s.at[at], y_r.at[at], peer(dy=step))

    def y_arrival(direction, hop, p):
        step = 1 if direction == UP else -1
        yb = wrap(y - step * hop, NY)
        view = tokv.at[tok_rows(yb, c, p), :]
        at = (direction, hop - 1, p)
        return yb, copy(view, view, y_s.at[at], y_r.at[at], peer(dy=step))

    def to_sibling(n, p):
        yb = wrap(y + REL[n], NY)
        view = tokv.at[tok_rows(yb, c, p), :]
        start(copy(view, view, c_s.at[n, p], c_r.at[n, p], peer(dc=1)))

    def y_recv(direction, hop, p):
        _, cp = y_arrival(direction, hop, p)
        cp.wait_recv()
        if hop < 3 or (hop == 3 and p == direction):
            start(y_copy(direction, hop + 1, p))
        step = 1 if direction == UP else -1
        n = REL.index(-step * hop) if hop < 4 else 7
        to_sibling(n, p)

    def x_weights():
        for k in range(1, NX):
            view = wx.at[wx_rows(x), :]
            start(copy(view, view, w_s.at[k], w_r.at[k], peer(dx=k)))

    def x_weights_recv():
        for k in range(1, NX):
            view = wx.at[wx_rows(wrap(x - k, NX)), :]
            copy(view, view, w_s.at[k], w_r.at[k], peer(dx=k)).wait_recv()
        pick = jnp.where(
            lax.broadcasted_iota(jnp.int32, (ZBLK, NX * WBLK), 0) == lay_ref[5:6, 0 : NX * WBLK],
            1.0,
            0.0,
        ).astype(BF16)
        wst[pl.ds(aligned(z * ZBLK, 16), ZBLK), :] = dot(pick, wx[...]).astype(BF16)
        for p in range(2):
            for direction in (UP, DOWN):
                start(z_copy(direction, 1, p))

    def z_view(zb, p):
        first, count = ZPIECES[p]
        return wst.at[pl.ds(aligned(zb * ZBLK + first, 16), count), :]

    def z_copy(direction, hop, p):
        step = 1 if direction == UP else -1
        view = z_view(wrap(z - step * (hop - 1), NZ), p)
        at = (direction, hop - 1, p)
        return copy(view, view, z_s.at[at], z_r.at[at], peer(dz=step))

    def z_recv(direction, hop, p):
        step = 1 if direction == UP else -1
        view = z_view(wrap(z - step * hop, NZ), p)
        at = (direction, hop - 1, p)
        copy(view, view, z_s.at[at], z_r.at[at], peer(dz=step)).wait_recv()
        if hop < 3 or (hop == 3 and p == direction):
            start(z_copy(direction, hop + 1, p))

    def z_both(hop, p):
        z_recv(UP, hop, p)
        z_recv(DOWN, hop, p)

    def up_grad():
        def tile(t, carry):
            rows = pl.ds(aligned(t * 64, 64), 64)
            g = gate_ref[rows, :].astype(F32)
            a = adj_ref[rows, :].astype(F32)
            u_ref[rows, :] = (a * (g / (1.0 + jnp.exp(-g)))).astype(BF16)
            return carry

        lax.fori_loop(0, FF // 64, tile, 0)

    def to_owner(l, make):
        k = wrap(x - 2 * c - l, NX)

        @pl.when(k != 0)
        def _():
            make(k, ((z * NX + 2 * c + l), me)).start()

    def u_copy(l):
        def make(k, device):
            return copy(
                uown.at[l, :, pl.ds(0, 256)],
                ucat.at[:, pl.ds(aligned(k * DEPTH, DEPTH), 256)],
                uc_s.at[l, 0],
                uc_r.at[k, 0],
                device,
            )

        return make

    def u_tail_copy(l):
        def make(k, device):
            return copy(utail.at[l], utails.at[k], uc_s.at[l, 1], uc_r.at[k, 1], device)

        return make

    def unpack(k):
        lane = lax.broadcasted_iota(jnp.int32, (HALF, 128), 1)
        both = utails[k].astype(F32)
        for t in range(2):
            moved = both if t == 0 else jnp.concatenate([both[:, 64:], both[:, :64]], axis=1)
            ucat[t * HALF : (t + 1) * HALF, k * DEPTH + 256 : (k + 1) * DEPTH] = jnp.where(
                lane < 64, moved, 0.0
            ).astype(BF16)

    def s_copy(l, g):
        def make(k, device):
            return copy(
                sown.at[l, pl.ds(g * GROUP, GROUP), :],
                scat.at[pl.ds(aligned(k * DEPTH + g * GROUP, 16), GROUP), :],
                sc_s.at[l, g],
                sc_r.at[k, g],
                device,
            )

        return make

    def expert_major():
        chip = jnp.bitwise_and(lay_ref[0:1, 0:DEPTH] + y, NY - 1)
        for l in range(2):
            source = chip * (4 * CAP) + lay_ref[1:2, 0:DEPTH] + l * CAP
            pick = jnp.where(
                lax.broadcasted_iota(jnp.int32, (SLOTS, DEPTH), 0) == source, 1.0, 0.0
            ).astype(BF16)
            tails = []
            for t in range(2):
                rows = slice(t * HALF, (t + 1) * HALF)
                full = dot(u_ref[rows, :], pick)
                uown[l, rows, :] = full.astype(BF16)
                tails.append(full[:, 256 : 256 + 64])
            utail[l] = jnp.concatenate(tails, axis=1).astype(BF16)
            to_owner(l, u_copy(l))
            to_owner(l, u_tail_copy(l))

    def source_major():
        row = lax.broadcasted_iota(jnp.int32, (SLOTS, SLOTS), 0)
        col = lax.broadcasted_iota(jnp.int32, (SLOTS, SLOTS), 1)
        utj[...] = dot_nt(jnp.where(row == col, 1.0, 0.0).astype(BF16), u_ref[...]).astype(BF16)

    def stacked(t):
        cols = slice(t * 512, min((t + 1) * 512, WALL))
        width = cols.stop - cols.start
        pick = jnp.where(
            lax.broadcasted_iota(jnp.int32, (FF, width), 0) == lay_ref[3:4, cols], 1.0, 0.0
        ).astype(BF16)
        which = lay_ref[4:5, cols]
        tile = 8 * CAP
        row = lax.broadcasted_iota(jnp.int32, (tile, width), 0)
        row_expert = jnp.zeros((tile, width), jnp.int32)
        for edge in range(1, 8):
            row_expert = jnp.where(row >= edge * CAP, edge % 2, row_expert)
        keep = row_expert == which
        full = dot(utj[...], pick)
        for first in range(0, SLOTS, tile):
            rows = slice(first, first + tile)
            ustt[rows, cols] = jnp.where(keep, full[rows, :], 0.0).astype(BF16)

    def gather(g):
        chips = [wrap(y + REL[n], NY) for n in (2 * g, 2 * g + 1)]
        for n, yb in zip((2 * g, 2 * g + 1), chips):
            for p in range(2):
                view = tokv.at[tok_rows(yb, 1 - c, p), :]
                copy(view, view, c_s.at[n, p], c_r.at[n, p], peer(dc=1)).wait_recv()
        far = 1 << 12
        codes = []
        for b in range(4):
            codes.append(tbl[chips[b // 2] * 2 + b % 2] + b * far)
        codes = jnp.concatenate(codes, axis=1)
        row = lax.broadcasted_iota(jnp.int32, (GROUP, 4 * TOK), 0)
        want = row
        for b in range(1, 4):
            want = jnp.where(row >= b * CAP, row + b * (far - CAP), want)
        hits = []
        for l in range(2):
            base = want + (2 * me + l) * 32
            hit = jnp.zeros((GROUP, 4 * TOK), F32)
            for k in range(TOP):
                hit = hit + jnp.where(codes[k : k + 1, :] == base, 1.0, 0.0)
            hits.append(hit)
        pick = jnp.concatenate(hits, axis=0).astype(BF16)
        got = jnp.zeros((2 * GROUP, D), F32)
        for i in range(2):
            tokens = tokv[pl.ds(aligned(chips[i] * 2 * TOK, 2 * TOK), 2 * TOK), :]
            got = got + dot(pick[:, i * 2 * TOK : (i + 1) * 2 * TOK], tokens)
        got = got.astype(BF16)
        for l in range(2):
            sown[l, g * GROUP : (g + 1) * GROUP, :] = got[l * GROUP : (l + 1) * GROUP, :]
            to_owner(l, s_copy(l, g))

        @pl.when(is_owner)
        def _():
            scat[g * GROUP : (g + 1) * GROUP, :] = sown[l_own, g * GROUP : (g + 1) * GROUP, :]

    for i in range(1, NE):
        j = lax.rem(me + i, NE)
        start(copy(tbl.at[me], tbl.at[me], t_s.at[i], t_r.at[i], (dp, j)))
    for p in range(2):
        for direction in (UP, DOWN):
            start(y_copy(direction, 1, p))
    x_weights()
    for p in range(2):
        to_sibling(0, p)

    def y_both(hop, p):
        y_recv(UP, hop, p)
        y_recv(DOWN, hop, p)

    for cp in loads[4:]:
        cp.wait()
    up_grad()
    expert_major()
    y_both(1, 0)
    x_weights_recv()
    y_both(1, 1)
    for i in range(1, NE):
        j = lax.rem(me + NE - i, NE)
        copy(tbl.at[j], tbl.at[j], t_s.at[i], t_r.at[i], (dp, j)).wait_recv()
    gather(0)
    source_major()
    y_both(2, 0)
    stacked(0)
    z_both(1, 0)
    y_both(2, 1)
    gather(1)
    stacked(1)
    y_both(3, 0)
    z_both(1, 1)
    stacked(2)
    y_both(3, 1)
    gather(2)
    z_both(2, 0)
    y_recv(UP, 4, 0)
    y_recv(DOWN, 4, 1)
    gather(3)
    z_both(2, 1)
    z_both(3, 0)

    z2 = z // 2
    order = [wrap(z2 + k, 4) for k in (2, 1, 3, 0)]

    def cols2(i):
        return pl.ds(aligned(order[i] * 256, 256), 256)

    def z_part(i, k):
        zeta = order[i] * 2 + k
        view = zsend.at[:, pl.ds(aligned(zeta * 128, 128), 128)]
        return copy(view, zrecv.at[z], zp_s.at[i, k], zp_r.at[z], (zeta * NX + x, me))

    @pl.when(is_owner)
    def _():
        ucat[:, 0:DEPTH] = uown[l_own]
        for k in range(1, NX):
            view = ucat.at[:, pl.ds(k * DEPTH, 256)]
            copy(view, view, uc_s.at[0, 0], uc_r.at[k, 0], peer(dx=k)).wait_recv()
            view = utails.at[k]
            copy(view, view, uc_s.at[0, 1], uc_r.at[k, 1], peer(dx=k)).wait_recv()
            unpack(k)
        for g in range(4):
            for k in range(1, NX):
                view = scat.at[pl.ds(k * DEPTH + g * GROUP, GROUP), :]
                copy(view, view, sc_s.at[0, 0], sc_r.at[k, g], peer(dx=k)).wait_recv()
        for i in range(4):
            halves = []
            for t in range(2):
                rows = slice(t * HALF, (t + 1) * HALF)
                halves.append(dot(ucat[rows, :], scat[:, cols2(i)]))
                zsend[rows, cols2(i)] = halves[t].astype(BF16)
            if i < 3:
                z_part(i, 0).start()
                z_part(i, 1).start()
            else:

                @pl.when(lax.rem(z, 2) == 0)
                def _():
                    z_part(i, 1).start()
                    for t in range(2):
                        zown[t * HALF : (t + 1) * HALF, :] = halves[t][:, 0:128]

                @pl.when(lax.rem(z, 2) == 1)
                def _():
                    z_part(i, 0).start()
                    for t in range(2):
                        zown[t * HALF : (t + 1) * HALF, :] = halves[t][:, 128:256]

    def slot_grads(n):
        cols = slice(n * 256, (n + 1) * 256)
        sg[:, cols] = dot(ustt[...], wst[:, cols]).astype(BF16)

    def chip_rows(yb):
        return pl.ds(aligned(yb * GROUP, 16), GROUP)

    z_both(3, 1)
    z_recv(UP, 4, 0)
    z_recv(DOWN, 4, 1)
    for n in range(4):
        slot_grads(n)
    for k in (4, 3, 5, 2, 6, 1, 7):
        yb = wrap(y + k, NY)
        start(
            copy(
                sg.at[chip_rows(yb), :],
                ret.at[chip_rows(y), :],
                rt_s.at[k],
                rt_r.at[k],
                (dp, yb * 2 + c),
            )
        )
    ret[chip_rows(y), :] = sg[chip_rows(y), :]

    codes = jnp.concatenate([tbl[2 * y], tbl[2 * y + 1] + (1 << 12)], axis=1)
    row = lax.broadcasted_iota(jnp.int32, (GROUP, 2 * TOK), 0)
    want = row
    for b in range(1, 4):
        want = jnp.where(row >= b * CAP, row + (b // 2) * (1 << 12) + (b % 2) * 32 - b * CAP, want)
    picks = []
    for yb in range(NY):
        base = want + (yb * 4 + 2 * c) * 32
        hit = jnp.zeros((GROUP, 2 * TOK), F32)
        for k in range(TOP):
            hit = hit + jnp.where(codes[k : k + 1, :] == base, 1.0, 0.0)
        picks.append(hit)
    picked[...] = jnp.concatenate(picks, axis=0).T.astype(BF16)

    zcols = pl.ds(aligned(z * 128, 128), 128)

    def ag_view(zb, p):
        return grad.at[pl.ds(p * HALF, HALF), pl.ds(aligned(zb * 128, 128), 128)]

    def ag_copy(direction, hop, p):
        step = 1 if direction == UP else -1
        view = ag_view(wrap(z - step * (hop - 1), NZ), p)
        at = (direction, hop - 1, p)
        return copy(view, view, ag_s.at[at], ag_r.at[at], peer(dz=step))

    def ag_recv(direction, hop, p):
        step = 1 if direction == UP else -1
        view = ag_view(wrap(z - step * hop, NZ), p)
        at = (direction, hop - 1, p)
        copy(view, view, ag_s.at[at], ag_r.at[at], peer(dz=step)).wait_recv()
        if hop < 3 or (hop == 3 and p == direction):
            ag_copy(direction, hop + 1, p).start()

    def rows_copy(k):
        xd = wrap(x + k, NX)
        return copy(
            rows_ref.at[pl.ds(aligned(xd * 32, 32), 32), :],
            fin.at[l_own],
            fn_s.at[k],
            fn_r.at[l_own],
            peer(dx=k),
        )

    @pl.when(is_owner)
    def _():
        total = zown[...]
        for k in range(1, NZ):
            src = wrap(z + k, NZ)
            view = zrecv.at[src]
            copy(view, view, zp_s.at[0, 0], zp_r.at[src], peer(dz=k)).wait_recv()
            total = total + zrecv[src].astype(F32)
        grad[:, zcols] = total.astype(BF16)
        for p in range(2):
            for direction in (UP, DOWN):
                ag_copy(direction, 1, p).start()
        squares = jnp.zeros((1, 256), F32)
        for hop in range(1, 5):
            if hop < 4:
                for p in range(2):
                    for direction in (UP, DOWN):
                        ag_recv(direction, hop, p)
                pair = (z - hop, z + hop)
            else:
                ag_recv(UP, 4, 0)
                ag_recv(DOWN, 4, 1)
                pair = (z + 4, z)
            both = jnp.concatenate(
                [grad[:, pl.ds(aligned(wrap(zb, NZ) * 128, 128), 128)] for zb in pair], axis=1
            )
            wide = both.astype(F32)
            squares = squares + jnp.sum(wide * wide, axis=0, keepdims=True)
            for t in range(2):
                rows = slice(t * HALF, (t + 1) * HALF)
                term = dot_nt(both[rows, :], both)
                gram_sum[rows, :] = term if hop == 1 else gram_sum[rows, :] + term
        norm = jnp.sqrt(jnp.sum(squares, axis=1, keepdims=True))
        inverse = 1.0 / (norm + EPSILON)
        gram[...] = (gram_sum[...] * inverse * inverse).astype(BF16)

        halves = [slice(0, HALF), slice(HALF, FF)]
        for rows in halves:
            square = dot(gram[rows, :], gram[...])
            poly[rows, :] = (QUINT_B * gram[rows, :].astype(F32) + QUINT_C * square).astype(BF16)
        for rows in halves:
            x1_ref[rows, :] = (
                inverse * (QUINT_A * grad[rows, :].astype(F32) + dot(poly[rows, :], grad[...]))
            ).astype(BF16)
        for rows in halves:
            gram[rows, :] = dot_nt(x1_ref[rows, :], x1_ref[...]).astype(BF16)
        picks = []
        for xd in range(NX):
            r = lax.broadcasted_iota(jnp.int32, (32, FF), 0)
            f = lax.broadcasted_iota(jnp.int32, (32, FF), 1)
            hit = jnp.logical_and(r < ROWS, f == r + (z * NX + xd) * ROWS)
            picks.append(jnp.where(hit, 1.0, 0.0))
        pick = jnp.concatenate(picks, axis=0).astype(BF16)
        gram_rows = dot(pick, gram[...]).astype(BF16)
        it_rows = dot(pick, x1_ref[...])
        poly_rows = (QUINT_B * gram_rows.astype(F32) + QUINT_C * dot(gram_rows, gram[...])).astype(
            BF16
        )
        rows_ref[...] = (QUINT_A * it_rows + dot(poly_rows, x1_ref[...])).astype(BF16)
        for k in range(1, NX):
            rows_copy(k).start()
        fin[l_own] = rows_ref[pl.ds(aligned(x * 32, 32), 32), :]

    for k in range(1, NY):
        view = ret.at[chip_rows(wrap(y - k, NY)), :]
        copy(view, view, rt_s.at[k], rt_r.at[k], peer(dy=k)).wait_recv()

    def core_rows(core):
        return pl.ds(aligned(core * TOK, TOK), TOK)

    for_sibling[...] = dot(picked[core_rows(1 - c), :], ret[...])
    sibling = copy(for_sibling, from_sibling, sib_s, sib_r, peer(dc=1))
    start(sibling)
    mine = dot(picked[core_rows(c), :], ret[...])
    sibling.wait_recv()
    out_tok[...] = (mine + from_sibling[...]).astype(BF16)

    scale = 0.2 * math.sqrt(max(FF, D))
    for l in range(2):
        owner_x = 2 * c + l

        @pl.when(x != owner_x)
        def _():
            view = fin.at[l]
            copy(view, view, fn_s.at[1], fn_r.at[l], peer(dx=1)).wait_recv()

        out_mu[:, l, :] = scale * fin[l, 0:ROWS, :].astype(F32)

    for cp in sent:
        cp.wait_send()

    for l in range(2):
        k = wrap(x - 2 * c - l, NX)

        @pl.when(k != 0)
        def _():
            device = (z * NX + 2 * c + l, me)
            u_copy(l)(k, device).wait_send()
            u_tail_copy(l)(k, device).wait_send()
            for g in range(4):
                s_copy(l, g)(k, device).wait_send()

    @pl.when(is_owner)
    def _():
        for i in range(3):
            z_part(i, 0).wait_send()
            z_part(i, 1).wait_send()

        @pl.when(lax.rem(z, 2) == 0)
        def _():
            z_part(3, 1).wait_send()

        @pl.when(lax.rem(z, 2) == 1)
        def _():
            z_part(3, 0).wait_send()

        for hop in range(1, 5):
            for p in range(2):
                for direction in (UP, DOWN):
                    if hop < 4 or p == direction:
                        ag_copy(direction, hop, p).wait_send()
        for k in range(1, NX):
            rows_copy(k).wait_send()


def body(tokens, weights, gate, adjoint, chosen, seat, quota):
    vmem = pl.BlockSpec(memory_space=pltpu.VMEM)
    anywhere = pl.BlockSpec(memory_space=pl.ANY)
    sem = pltpu.SemaphoreType.DMA
    scratch = [
        pltpu.VMEM((ROWS, 2, D), BF16),
        pltpu.VMEM((FF, SLOTS), BF16),
        pltpu.VMEM((FF, SLOTS), BF16),
        pltpu.VMEM((TOP, TOK), jnp.int32),
        pltpu.VMEM((TOP, TOK), jnp.int32),
        pltpu.VMEM((8, WALL), jnp.int32),
        sem((7,)),
        pltpu.VMEM((NE * TOK, D), BF16),
        pltpu.VMEM((NX * WBLK, D), BF16),
        pltpu.VMEM((WALL, D), BF16),
        pltpu.VMEM((NE, 8, TOK), jnp.int32),
        pltpu.VMEM((FF, SLOTS), BF16),
        pltpu.VMEM((2, FF, DEPTH), BF16),
        pltpu.VMEM((2, HALF, 128), BF16),
        pltpu.VMEM((NX, HALF, 128), BF16),
        pltpu.VMEM((FF, NX * DEPTH), BF16),
        pltpu.VMEM((SLOTS, FF), BF16),
        pltpu.VMEM((SLOTS, WALL), BF16),
        pltpu.VMEM((2, SLOTS_E, D), BF16),
        pltpu.VMEM((NX * DEPTH, D), BF16),
        pltpu.VMEM((FF, D), BF16),
        pltpu.VMEM((FF, 128), F32),
        pltpu.VMEM((NZ, FF, 128), BF16),
        pltpu.VMEM((SLOTS, D), BF16),
        pltpu.VMEM((SLOTS, D), BF16),
        pltpu.VMEM((FF, D), BF16),
        pltpu.VMEM((FF, D), BF16),
        pltpu.VMEM((FF, FF), F32),
        pltpu.VMEM((FF, FF), BF16),
        pltpu.VMEM((FF, FF), BF16),
        pltpu.VMEM((128, D), BF16),
        pltpu.VMEM((2, 32, D), BF16),
        sem((NE,)),
        sem((NE,)),
        sem((2, 4, 2)),
        sem((2, 4, 2)),
        sem((8, 2)),
        sem((8, 2)),
        sem((NX,)),
        sem((NX,)),
        sem((2, 4, 2)),
        sem((2, 4, 2)),
        sem((2, 2)),
        sem((NX, 2)),
        sem((2, 4)),
        sem((NX, 4)),
        sem((4, 2)),
        sem((NZ,)),
        sem((2, 4, 2)),
        sem((2, 4, 2)),
        sem((NY,)),
        sem((NY,)),
        sem((NX,)),
        sem((2,)),
        pltpu.VMEM((2 * TOK, SLOTS), BF16),
        pltpu.VMEM((TOK, D), F32),
        pltpu.VMEM((TOK, D), F32),
        sem,
        sem,
    ]
    return pl.pallas_call(
        kernel,
        out_shape=(
            jax.ShapeDtypeStruct((TOK, D), BF16),
            jax.ShapeDtypeStruct((ROWS, 2, D), F32),
        ),
        in_specs=[anywhere] * 6 + [pl.BlockSpec(memory_space=pltpu.SMEM), anywhere],
        out_specs=(vmem, vmem),
        scratch_shapes=scratch,
        compiler_params=pltpu.CompilerParams(
            collective_id=0, has_side_effects=True, vmem_limit_bytes=60 * 2**20
        ),
        cost_estimate=pl.CostEstimate(
            flops=16 * 10**9, bytes_accessed=5 * 10**6, transcendentals=450560
        ),
        name="expert_backward",
    )(tokens, weights, gate, adjoint, chosen.T, seat.T, quota, jnp.asarray(layout_tables()))


def solution(mesh):
    return jax.shard_map(
        body,
        mesh=mesh,
        in_specs=(
            P(("dp", "expert"), None),
            P("dp", "expert", None),
            P(None, ("dp", "expert")),
            P(None, ("dp", "expert")),
            P(("dp", "expert"), None),
            P(("dp", "expert"), None),
            P(),
        ),
        out_specs=(P(("dp", "expert"), None), P("dp", "expert", None)),
        check_vma=False,
    )
```

```python
import math

import jax
import jax.numpy as jnp
import numpy as np
from jax import lax
from jax.experimental import pallas as pl
from jax.experimental.pallas import tpu as pltpu
from jax.sharding import PartitionSpec as P

MESH = pl.DeviceIdType.MESH
F32 = jnp.float32
BF16 = jnp.bfloat16

ITERS = 2
QUINT_A = 3.4445
QUINT_B = -4.775
QUINT_C = 2.0315
EPSILON = 1e-06

NX, NY, NZ = 4, 8, 8
NE = 2 * NY
FF, D = 704, 1024
TOK, TOP = 128, 6
CAP = 20
SLOTS = 2 * NE * CAP
ROWS = FF // (NX * NZ)
WPAD = 32
GROUP = 4 * CAP
SLOTS_E = NE * CAP
DEPTH = 384
ZROWS = NX * ROWS
ZBLK = 96
ZPIECES = ((0, 48), (48, 48))
REL = (0, -1, 1, -2, 2, -3, 3, 4)
HALF = FF // 2
PART = FF // 4
PIECE = TOK // 2

UP, DOWN = 0, 1


def layout_tables():
    table = np.full((8, DEPTH), -1, np.int32)
    table[1, :] = -(1 << 20)
    for n in range(NY):
        for core in range(2):
            for p in range(CAP):
                at = (n * 2 + core) * CAP + p
                table[0, at] = REL[n] % NY
                table[1, at] = core * 2 * CAP + p
    for k in range(NX):
        for i in range(ROWS):
            table[2, k * WPAD + i] = k * ROWS + i
    return table


def dot(a, b):
    return jnp.dot(a, b, preferred_element_type=F32)


def dot_nt(a, b):
    return lax.dot_general(a, b, (((1,), (1,)), ((), ())), preferred_element_type=F32)


def kernel(
    tok_hbm,
    w_hbm,
    gate_hbm,
    adj_hbm,
    chosen_hbm,
    seat_hbm,
    quota_ref,
    lay_hbm,
    out_tok,
    out_mu,
    w_ref,
    gate_ref,
    adj_ref,
    chosen_ref,
    seat_ref,
    lay_ref,
    in_s,
    tokv,
    wsend,
    wx,
    wst,
    tbl,
    u_ref,
    uown,
    utail,
    utails,
    ucat,
    ut,
    wnat,
    sown,
    scat,
    zsend,
    zown,
    near,
    third,
    fourth,
    far,
    sg,
    sgl,
    sgo,
    ret,
    grad,
    x1_ref,
    gram_sum,
    gram,
    poly,
    rows_ref,
    fin,
    t_s,
    t_r,
    y_s,
    y_r,
    c_s,
    c_r,
    w_s,
    w_r,
    z_s,
    z_r,
    uc_s,
    uc_r,
    sc_s,
    sc_r,
    sg_s,
    sg_r,
    nr_s,
    nr_r,
    th_s,
    th_r,
    fo_s,
    fo_r,
    fr_s,
    fr_r,
    ag_s,
    ag_r,
    rt_s,
    rt_r,
    fn_s,
    fn_r,
    picked,
    for_sibling,
    from_sibling,
    sib_s,
    sib_r,
):
    dp = lax.axis_index("dp")
    me = lax.axis_index("expert")
    x, z = lax.rem(dp, NX), dp // NX
    y, c = me // 2, lax.rem(me, 2)

    def wrap(v, n):
        return lax.rem(v + 2 * n, n)

    def peer(dx=0, dy=0, dz=0, dc=0):
        core = lax.rem(c + dc, 2)
        return (wrap(z + dz, NZ) * NX + wrap(x + dx, NX), wrap(y + dy, NY) * 2 + core)

    def copy(ref_src, ref_dst, ssem, rsem, device):
        return pltpu.make_async_remote_copy(
            src_ref=ref_src,
            dst_ref=ref_dst,
            send_sem=ssem,
            recv_sem=rsem,
            device_id=device,
            device_id_type=MESH,
        )

    def aligned(v, m):
        return pl.multiple_of(v, m)

    barrier = pltpu.get_barrier_semaphore()
    greeted = [(dp, lax.rem(me + i, NE)) for i in range(1, NE)]
    greeted += [peer(dz=k) for k in range(1, NZ)]
    greeted += [peer(dx=k) for k in range(1, NX)]
    for device in greeted:
        pl.semaphore_signal(barrier, inc=1, device_id=device, device_id_type=MESH)

    own_rows = pl.ds(aligned(y * (2 * TOK) + c * TOK, TOK), TOK)
    operands = (
        (tok_hbm, tokv.at[own_rows, :]),
        (w_hbm, w_ref),
        (chosen_hbm, chosen_ref),
        (seat_hbm, seat_ref),
        (lay_hbm, lay_ref),
        (gate_hbm, gate_ref),
        (adj_hbm, adj_ref),
    )
    loads = [pltpu.make_async_copy(a, b, in_s.at[i]) for i, (a, b) in enumerate(operands)]
    for cp in loads:
        cp.start()
    for cp in loads[:4]:
        cp.wait()

    chosen = chosen_ref[...]
    quota = jnp.zeros_like(chosen)
    for e in range(2 * NE):
        quota = jnp.where(chosen == e, quota_ref[e], quota)
    code = jnp.where(seat_ref[...] < quota, chosen * 32 + seat_ref[...], -1)
    tbl[me, 0:TOP, :] = code
    tbl[me, TOP:8, :] = jnp.full((8 - TOP, TOK), -1, jnp.int32)

    def tok_rows(yb, cb, p):
        return pl.ds(aligned(yb * (2 * TOK) + cb * TOK + p * PIECE, PIECE), PIECE)

    def wx_rows(xb):
        return pl.ds(aligned(xb * WPAD, WPAD), WPAD)

    blank = jnp.zeros((WPAD - ROWS, D), BF16)
    for l in range(2):
        wsend[l] = jnp.concatenate([w_ref[:, l, :], blank], axis=0)
    for k in range(NX):
        scat[k * DEPTH + SLOTS_E : (k + 1) * DEPTH, :] = jnp.zeros((DEPTH - SLOTS_E, D), BF16)

    r0 = wrap(x - 2 * c, NX)
    is_owner = r0 < 2
    l_own = lax.rem(r0, 2)

    pl.semaphore_wait(barrier, len(greeted))

    sent = []

    def start(cp):
        cp.start()
        sent.append(cp)

    def y_copy(direction, hop, p):
        step = 1 if direction == UP else -1
        yb = wrap(y - step * (hop - 1), NY)
        view = tokv.at[tok_rows(yb, c, p), :]
        at = (direction, hop - 1, p)
        return copy(view, view, y_s.at[at], y_r.at[at], peer(dy=step))

    def y_arrival(direction, hop, p):
        step = 1 if direction == UP else -1
        yb = wrap(y - step * hop, NY)
        view = tokv.at[tok_rows(yb, c, p), :]
        at = (direction, hop - 1, p)
        return yb, copy(view, view, y_s.at[at], y_r.at[at], peer(dy=step))

    def to_sibling(n, p):
        yb = wrap(y + REL[n], NY)
        view = tokv.at[tok_rows(yb, c, p), :]
        start(copy(view, view, c_s.at[n, p], c_r.at[n, p], peer(dc=1)))

    def y_recv(direction, hop, p):
        _, cp = y_arrival(direction, hop, p)
        cp.wait_recv()
        if hop < 3 or (hop == 3 and p == direction):
            start(y_copy(direction, hop + 1, p))
        step = 1 if direction == UP else -1
        n = REL.index(-step * hop) if hop < 4 else 7
        to_sibling(n, p)

    def to_owner(l, make):
        k = wrap(x - 2 * c - l, NX)

        @pl.when(k != 0)
        def _():
            make(k, ((z * NX + 2 * c + l), me)).start()

    def w_copy(l):
        def make(k, device):
            return copy(wsend.at[l], wx.at[wx_rows(x), :], w_s.at[l], w_r.at[k], device)

        return make

    def x_weights():
        for l in range(2):
            to_owner(l, w_copy(l))

    def x_weights_recv():
        wx[wx_rows(x), :] = wsend[l_own]
        for k in range(1, NX):
            view = wx.at[wx_rows(wrap(x + k, NX)), :]
            copy(view, view, w_s.at[0], w_r.at[k], peer(dx=k)).wait_recv()
        pick = jnp.where(
            lax.broadcasted_iota(jnp.int32, (ZBLK, NX * WPAD), 0) == lay_ref[2:3, 0 : NX * WPAD],
            1.0,
            0.0,
        ).astype(BF16)
        wst[pl.ds(aligned(z * ZBLK, 16), ZBLK), :] = dot(pick, wx[...]).astype(BF16)
        for p in range(2):
            for direction in (UP, DOWN):
                z_copy(direction, 1, p).start()

    def z_view(zb, p):
        first, count = ZPIECES[p]
        return wst.at[pl.ds(aligned(zb * ZBLK + first, 16), count), :]

    def z_copy(direction, hop, p):
        step = 1 if direction == UP else -1
        view = z_view(wrap(z - step * (hop - 1), NZ), p)
        at = (direction, hop - 1, p)
        return copy(view, view, z_s.at[at], z_r.at[at], peer(dz=step))

    def z_recv(direction, hop, p):
        step = 1 if direction == UP else -1
        view = z_view(wrap(z - step * hop, NZ), p)
        at = (direction, hop - 1, p)
        copy(view, view, z_s.at[at], z_r.at[at], peer(dz=step)).wait_recv()
        if hop < 3 or (hop == 3 and p == direction):
            z_copy(direction, hop + 1, p).start()

    def z_both(hop, p):
        z_recv(UP, hop, p)
        z_recv(DOWN, hop, p)

    def up_grad():
        def tile(t, carry):
            rows = pl.ds(aligned(t * 64, 64), 64)
            g = gate_ref[rows, :].astype(F32)
            a = adj_ref[rows, :].astype(F32)
            u_ref[rows, :] = (a * (g / (1.0 + jnp.exp(-g)))).astype(BF16)
            return carry

        lax.fori_loop(0, FF // 64, tile, 0)

    def u_copy(l):
        def make(k, device):
            return copy(
                uown.at[l, :, pl.ds(0, 256)],
                ucat.at[:, pl.ds(aligned(k * DEPTH, DEPTH), 256)],
                uc_s.at[l, 0],
                uc_r.at[k, 0],
                device,
            )

        return make

    def u_tail_copy(l):
        def make(k, device):
            return copy(utail.at[l], utails.at[k], uc_s.at[l, 1], uc_r.at[k, 1], device)

        return make

    def unpack(k):
        lane = lax.broadcasted_iota(jnp.int32, (HALF, 128), 1)
        both = utails[k].astype(F32)
        for t in range(2):
            moved = both if t == 0 else jnp.concatenate([both[:, 64:], both[:, :64]], axis=1)
            ucat[t * HALF : (t + 1) * HALF, k * DEPTH + 256 : (k + 1) * DEPTH] = jnp.where(
                lane < 64, moved, 0.0
            ).astype(BF16)

    def s_copy(l, g):
        def make(k, device):
            return copy(
                sown.at[l, pl.ds(g * GROUP, GROUP), :],
                scat.at[pl.ds(aligned(k * DEPTH + g * GROUP, 16), GROUP), :],
                sc_s.at[l, g],
                sc_r.at[k, g],
                device,
            )

        return make

    def expert_major():
        chip = jnp.bitwise_and(lay_ref[0:1, 0:DEPTH] + y, NY - 1)
        for l in range(2):
            source = chip * (4 * CAP) + lay_ref[1:2, 0:DEPTH] + l * CAP
            pick = jnp.where(
                lax.broadcasted_iota(jnp.int32, (SLOTS, DEPTH), 0) == source, 1.0, 0.0
            ).astype(BF16)
            tails = []
            for t in range(2):
                rows = slice(t * HALF, (t + 1) * HALF)
                full = dot(u_ref[rows, :], pick)
                uown[l, rows, :] = full.astype(BF16)
                tails.append(full[:, 256 : 256 + 64])
            utail[l] = jnp.concatenate(tails, axis=1).astype(BF16)
            to_owner(l, u_copy(l))
            to_owner(l, u_tail_copy(l))

    def u_recv():
        ucat[:, 0:DEPTH] = uown[l_own]
        for k in range(1, NX):
            view = ucat.at[:, pl.ds(k * DEPTH, 256)]
            copy(view, view, uc_s.at[0, 0], uc_r.at[k, 0], peer(dx=k)).wait_recv()
            view = utails.at[k]
            copy(view, view, uc_s.at[0, 1], uc_r.at[k, 1], peer(dx=k)).wait_recv()
            unpack(k)

    def transposed(k):
        row = lax.broadcasted_iota(jnp.int32, (SLOTS_E, DEPTH), 0)
        col = lax.broadcasted_iota(jnp.int32, (SLOTS_E, DEPTH), 1)
        same = jnp.where(row == col, 1.0, 0.0).astype(BF16)
        ut[k * SLOTS_E : (k + 1) * SLOTS_E, :] = dot_nt(
            same, ucat[:, k * DEPTH : (k + 1) * DEPTH]
        ).astype(BF16)

    def slot_grads():
        for zb in range(NZ):
            wnat[zb * ZROWS : (zb + 1) * ZROWS, :] = wst[zb * ZBLK : zb * ZBLK + ZROWS, :]
        for n in range(4):
            cols = slice(n * 256, (n + 1) * 256)
            sg[:, cols] = dot(ut[...], wnat[:, cols]).astype(BF16)

    def sg_copy(k, g):
        return copy(
            sg.at[pl.ds(k * SLOTS_E + g * GROUP, GROUP), :],
            sgl.at[l_own, pl.ds(g * GROUP, GROUP), :],
            sg_s.at[k, g],
            sg_r.at[l_own, g],
            peer(dx=k),
        )

    def gather(g):
        chips = [wrap(y + REL[n], NY) for n in (2 * g, 2 * g + 1)]
        for n, yb in zip((2 * g, 2 * g + 1), chips):
            for p in range(2):
                view = tokv.at[tok_rows(yb, 1 - c, p), :]
                copy(view, view, c_s.at[n, p], c_r.at[n, p], peer(dc=1)).wait_recv()
        far = 1 << 12
        codes = []
        for b in range(4):
            codes.append(tbl[chips[b // 2] * 2 + b % 2] + b * far)
        codes = jnp.concatenate(codes, axis=1)
        row = lax.broadcasted_iota(jnp.int32, (GROUP, 4 * TOK), 0)
        want = row
        for b in range(1, 4):
            want = jnp.where(row >= b * CAP, row + b * (far - CAP), want)
        hits = []
        for l in range(2):
            base = want + (2 * me + l) * 32
            hit = jnp.zeros((GROUP, 4 * TOK), F32)
            for k in range(TOP):
                hit = hit + jnp.where(codes[k : k + 1, :] == base, 1.0, 0.0)
            hits.append(hit)
        pick = jnp.concatenate(hits, axis=0).astype(BF16)
        got = jnp.zeros((2 * GROUP, D), F32)
        for i in range(2):
            tokens = tokv[pl.ds(aligned(chips[i] * 2 * TOK, 2 * TOK), 2 * TOK), :]
            got = got + dot(pick[:, i * 2 * TOK : (i + 1) * 2 * TOK], tokens)
        got = got.astype(BF16)
        for l in range(2):
            sown[l, g * GROUP : (g + 1) * GROUP, :] = got[l * GROUP : (l + 1) * GROUP, :]
            to_owner(l, s_copy(l, g))

        @pl.when(is_owner)
        def _():
            scat[g * GROUP : (g + 1) * GROUP, :] = sown[l_own, g * GROUP : (g + 1) * GROUP, :]

    for p in range(2):
        for direction in (UP, DOWN):
            start(y_copy(direction, 1, p))
    x_weights()
    for i in range(1, NE):
        j = lax.rem(me + i, NE)
        start(copy(tbl.at[me], tbl.at[me], t_s.at[i], t_r.at[i], (dp, j)))
    for p in range(2):
        to_sibling(0, p)

    def y_both(hop, p):
        y_recv(UP, hop, p)
        y_recv(DOWN, hop, p)

    for cp in loads[4:]:
        cp.wait()
    up_grad()
    expert_major()
    y_both(1, 0)

    @pl.when(is_owner)
    def _():
        x_weights_recv()

    y_both(1, 1)
    for i in range(1, NE):
        j = lax.rem(me + NE - i, NE)
        copy(tbl.at[j], tbl.at[j], t_s.at[i], t_r.at[i], (dp, j)).wait_recv()
    gather(0)

    @pl.when(is_owner)
    def _():
        z_both(1, 0)
        z_both(1, 1)

    y_both(2, 0)

    @pl.when(is_owner)
    def _():
        z_both(2, 0)
        z_both(2, 1)

    y_both(2, 1)
    gather(1)

    @pl.when(is_owner)
    def _():
        z_both(3, 0)
        z_both(3, 1)

    y_both(3, 0)

    @pl.when(is_owner)
    def _():
        u_recv()
        transposed(0)
        transposed(1)

    y_both(3, 1)
    gather(2)

    @pl.when(is_owner)
    def _():
        transposed(2)
        transposed(3)
        z_recv(UP, 4, 0)
        z_recv(DOWN, 4, 1)

    y_recv(UP, 4, 0)
    y_recv(DOWN, 4, 1)
    gather(3)

    @pl.when(is_owner)
    def _():
        slot_grads()
        for g in (3, 2, 1, 0):
            for k in range(1, NX):
                sg_copy(k, g).start()
        sgl[l_own] = sg[0:SLOTS_E, :]

    z2 = z // 2
    odd = lax.rem(z, 2)
    order = [wrap(z2 + k, 4) for k in (2, 1 + 2 * odd, 3 - 2 * odd, 0)]

    def cols2(i):
        return pl.ds(aligned(order[i] * 256, 256), 256)

    def zchunk(r):
        return pl.ds(aligned(wrap(z + r, NZ) * 128, 128), 128)

    def direct_copy(d):
        r, step = ((1, 1), (7, -1))[d]
        return copy(zsend.at[:, zchunk(r)], near.at[d], nr_s.at[d], nr_r.at[d], peer(dz=step))

    def third_copy(d):
        r, step = ((3, 1), (5, -1))[d]
        return copy(zsend.at[:, zchunk(r)], third.at[d], th_s.at[d], th_r.at[d], peer(dz=step))

    def fourth_copy(d):
        step = (2, -2)[d]
        rows = pl.ds(d * HALF, HALF)
        return copy(
            zsend.at[rows, zchunk(4)], fourth.at[d], fo_s.at[d], fo_r.at[d], peer(dz=step)
        )

    def relayed_copy(d):
        r, step = ((2, 2), (6, -2))[d]
        return copy(zsend.at[:, zchunk(r)], far.at[d], fr_s.at[d], fr_r.at[d], peer(dz=step))

    def relay(d):
        r = (2, 6)[d]
        third_copy(d).wait_recv()
        fourth_copy(d).wait_recv()
        for t in range(2):
            rows = slice(t * HALF, (t + 1) * HALF)
            total = zsend[rows, zchunk(r)].astype(F32) + third[d, rows, :].astype(F32)
            if t == d:
                total = total + fourth[d].astype(F32)
            zsend[rows, zchunk(r)] = total.astype(BF16)
        relayed_copy(d).start()

    @pl.when(is_owner)
    def _():
        for g in range(4):
            for k in range(1, NX):
                view = scat.at[pl.ds(k * DEPTH + g * GROUP, GROUP), :]
                copy(view, view, sc_s.at[0, 0], sc_r.at[k, g], peer(dx=k)).wait_recv()
        for i in range(4):
            halves = []
            for t in range(2):
                rows = slice(t * HALF, (t + 1) * HALF)
                halves.append(dot(ucat[rows, :], scat[:, cols2(i)]))
                zsend[rows, cols2(i)] = halves[t].astype(BF16)
            for parity in range(2):

                @pl.when(odd == parity)
                def _():
                    if i == 0:
                        fourth_copy(0).start()
                        fourth_copy(1).start()
                        third_copy(1 - parity).start()
                    elif i == 1:
                        third_copy(parity).start()
                    elif i == 2:
                        direct_copy(1 - parity).start()
                    else:
                        direct_copy(parity).start()
                        first = parity * 128
                        for t in range(2):
                            rows = slice(t * HALF, (t + 1) * HALF)
                            zown[rows, :] = halves[t][:, first : first + 128]

    def chip_rows(yb):
        return pl.ds(aligned(yb * GROUP, 16), GROUP)

    def return_copy(n):
        yb = wrap(y + REL[n], NY)
        return copy(
            sgo.at[pl.ds(n * GROUP, GROUP), :],
            ret.at[chip_rows(y), :],
            rt_s.at[n],
            rt_r.at[n],
            (dp, yb * 2 + c),
        )

    def send_back(g):
        for l in range(2):

            @pl.when(x != 2 * c + l)
            def _():
                view = sgl.at[l, pl.ds(g * GROUP, GROUP), :]
                copy(view, view, sg_s.at[1, g], sg_r.at[l, g], peer(dx=1)).wait_recv()

        for n in (2 * g + 1, 2 * g):
            both = [sgl[l, n * 2 * CAP : (n + 1) * 2 * CAP, :] for l in range(2)]
            sgo[n * GROUP : (n + 1) * GROUP, :] = jnp.concatenate(both, axis=0)
            if n:
                start(return_copy(n))

    send_back(3)
    send_back(2)

    @pl.when(is_owner)
    def _():
        relay(0)
        relay(1)

    send_back(1)
    send_back(0)
    ret[chip_rows(y), :] = sgo[0:GROUP, :]

    codes = jnp.concatenate([tbl[2 * y], tbl[2 * y + 1] + (1 << 12)], axis=1)
    row = lax.broadcasted_iota(jnp.int32, (GROUP, 2 * TOK), 0)
    want = row
    for b in range(1, 4):
        want = jnp.where(row >= b * CAP, row + (b % 2) * (1 << 12) + (b // 2) * 32 - b * CAP, want)
    picks = []
    for yb in range(NY):
        base = want + (yb * 4 + 2 * c) * 32
        hit = jnp.zeros((GROUP, 2 * TOK), F32)
        for k in range(TOP):
            hit = hit + jnp.where(codes[k : k + 1, :] == base, 1.0, 0.0)
        picks.append(hit)
    picked[...] = jnp.concatenate(picks, axis=0).T.astype(BF16)

    zcols = pl.ds(aligned(z * 128, 128), 128)

    def ag_view(zb, p):
        return grad.at[pl.ds(p * PART, PART), pl.ds(aligned(zb * 128, 128), 128)]

    def ag_copy(direction, hop, p):
        step = 1 if direction == UP else -1
        view = ag_view(wrap(z - step * (hop - 1), NZ), p)
        at = (direction, hop - 1, p)
        return copy(view, view, ag_s.at[at], ag_r.at[at], peer(dz=step))

    def ag_recv(direction, hop, p):
        step = 1 if direction == UP else -1
        view = ag_view(wrap(z - step * hop, NZ), p)
        at = (direction, hop - 1, p)
        copy(view, view, ag_s.at[at], ag_r.at[at], peer(dz=step)).wait_recv()
        if hop < 3 or (hop == 3 and p // 2 == direction):
            ag_copy(direction, hop + 1, p).start()

    def rows_copy(k):
        xd = wrap(x + k, NX)
        return copy(
            rows_ref.at[pl.ds(aligned(xd * 32, 32), 32), :],
            fin.at[l_own],
            fn_s.at[k],
            fn_r.at[l_own],
            peer(dx=k),
        )

    @pl.when(is_owner)
    def _():
        total = zown[...]
        for d in range(2):
            direct_copy(d).wait_recv()
            total = total + near[d].astype(F32)
        for d in range(2):
            relayed_copy(d).wait_recv()
            total = total + far[d].astype(F32)
        grad[:, zcols] = total.astype(BF16)
        for p in range(4):
            for direction in (UP, DOWN):
                ag_copy(direction, 1, p).start()
        squares = jnp.zeros((1, 256), F32)
        for hop in range(1, 5):
            if hop < 4:
                for p in range(4):
                    for direction in (UP, DOWN):
                        ag_recv(direction, hop, p)
                pair = (z - hop, z + hop)
            else:
                for p in range(2):
                    ag_recv(UP, 4, p)
                    ag_recv(DOWN, 4, 2 + p)
                pair = (z + 4, z)
            both = jnp.concatenate(
                [grad[:, pl.ds(aligned(wrap(zb, NZ) * 128, 128), 128)] for zb in pair], axis=1
            )
            wide = both.astype(F32)
            squares = squares + jnp.sum(wide * wide, axis=0, keepdims=True)
            for t in range(2):
                rows = slice(t * HALF, (t + 1) * HALF)
                term = dot_nt(both[rows, :], both)
                gram_sum[rows, :] = term if hop == 1 else gram_sum[rows, :] + term
        norm = jnp.sqrt(jnp.sum(squares, axis=1, keepdims=True))
        inverse = 1.0 / (norm + EPSILON)
        gram[...] = (gram_sum[...] * inverse * inverse).astype(BF16)

        halves = [slice(0, HALF), slice(HALF, FF)]
        for rows in halves:
            square = dot(gram[rows, :], gram[...])
            poly[rows, :] = (QUINT_B * gram[rows, :].astype(F32) + QUINT_C * square).astype(BF16)
        for rows in halves:
            x1_ref[rows, :] = (
                inverse * (QUINT_A * grad[rows, :].astype(F32) + dot(poly[rows, :], grad[...]))
            ).astype(BF16)
        for rows in halves:
            gram[rows, :] = dot_nt(x1_ref[rows, :], x1_ref[...]).astype(BF16)
        picks = []
        for xd in range(NX):
            r = lax.broadcasted_iota(jnp.int32, (32, FF), 0)
            f = lax.broadcasted_iota(jnp.int32, (32, FF), 1)
            hit = jnp.logical_and(r < ROWS, f == r + (z * NX + xd) * ROWS)
            picks.append(jnp.where(hit, 1.0, 0.0))
        pick = jnp.concatenate(picks, axis=0).astype(BF16)
        gram_rows = dot(pick, gram[...]).astype(BF16)
        it_rows = dot(pick, x1_ref[...])
        poly_rows = (QUINT_B * gram_rows.astype(F32) + QUINT_C * dot(gram_rows, gram[...])).astype(
            BF16
        )
        rows_ref[...] = (QUINT_A * it_rows + dot(poly_rows, x1_ref[...])).astype(BF16)
        for k in range(1, NX):
            rows_copy(k).start()
        fin[l_own] = rows_ref[pl.ds(aligned(x * 32, 32), 32), :]

    for n in range(1, NY):
        view = ret.at[chip_rows(wrap(y - REL[n], NY)), :]
        copy(view, view, rt_s.at[n], rt_r.at[n], peer(dy=-REL[n])).wait_recv()

    def core_rows(core):
        return pl.ds(aligned(core * TOK, TOK), TOK)

    for_sibling[...] = dot(picked[core_rows(1 - c), :], ret[...])
    sibling = copy(for_sibling, from_sibling, sib_s, sib_r, peer(dc=1))
    start(sibling)
    mine = dot(picked[core_rows(c), :], ret[...])
    sibling.wait_recv()
    out_tok[...] = (mine + from_sibling[...]).astype(BF16)

    scale = 0.2 * math.sqrt(max(FF, D))
    for l in range(2):
        owner_x = 2 * c + l

        @pl.when(x != owner_x)
        def _():
            view = fin.at[l]
            copy(view, view, fn_s.at[1], fn_r.at[l], peer(dx=1)).wait_recv()

        out_mu[:, l, :] = scale * fin[l, 0:ROWS, :].astype(F32)

    for cp in sent:
        cp.wait_send()

    for l in range(2):
        k = wrap(x - 2 * c - l, NX)

        @pl.when(k != 0)
        def _():
            device = (z * NX + 2 * c + l, me)
            w_copy(l)(k, device).wait_send()
            u_copy(l)(k, device).wait_send()
            u_tail_copy(l)(k, device).wait_send()
            for g in range(4):
                s_copy(l, g)(k, device).wait_send()

    @pl.when(is_owner)
    def _():
        for d in range(2):
            direct_copy(d).wait_send()
            third_copy(d).wait_send()
            fourth_copy(d).wait_send()
            relayed_copy(d).wait_send()

        for hop in range(1, 5):
            for p in range(2):
                for direction in (UP, DOWN):
                    if hop < 4 or p == direction:
                        z_copy(direction, hop, p).wait_send()
            for p in range(4):
                for direction in (UP, DOWN):
                    if hop < 4 or p // 2 == direction:
                        ag_copy(direction, hop, p).wait_send()
        for g in range(4):
            for k in range(1, NX):
                sg_copy(k, g).wait_send()
        for k in range(1, NX):
            rows_copy(k).wait_send()


def body(tokens, weights, gate, adjoint, chosen, seat, quota):
    vmem = pl.BlockSpec(memory_space=pltpu.VMEM)
    anywhere = pl.BlockSpec(memory_space=pl.ANY)
    sem = pltpu.SemaphoreType.DMA
    scratch = [
        pltpu.VMEM((ROWS, 2, D), BF16),
        pltpu.VMEM((FF, SLOTS), BF16),
        pltpu.VMEM((FF, SLOTS), BF16),
        pltpu.VMEM((TOP, TOK), jnp.int32),
        pltpu.VMEM((TOP, TOK), jnp.int32),
        pltpu.VMEM((8, DEPTH), jnp.int32),
        sem((7,)),
        pltpu.VMEM((NE * TOK, D), BF16),
        pltpu.VMEM((2, WPAD, D), BF16),
        pltpu.VMEM((NX * WPAD, D), BF16),
        pltpu.VMEM((NZ * ZBLK, D), BF16),
        pltpu.VMEM((NE, 8, TOK), jnp.int32),
        pltpu.VMEM((FF, SLOTS), BF16),
        pltpu.VMEM((2, FF, DEPTH), BF16),
        pltpu.VMEM((2, HALF, 128), BF16),
        pltpu.VMEM((NX, HALF, 128), BF16),
        pltpu.VMEM((FF, NX * DEPTH), BF16),
        pltpu.VMEM((NX * SLOTS_E, FF), BF16),
        pltpu.VMEM((FF, D), BF16),
        pltpu.VMEM((2, SLOTS_E, D), BF16),
        pltpu.VMEM((NX * DEPTH, D), BF16),
        pltpu.VMEM((FF, D), BF16),
        pltpu.VMEM((FF, 128), F32),
        pltpu.VMEM((2, FF, 128), BF16),
        pltpu.VMEM((2, FF, 128), BF16),
        pltpu.VMEM((2, HALF, 128), BF16),
        pltpu.VMEM((2, FF, 128), BF16),
        pltpu.VMEM((NX * SLOTS_E, D), BF16),
        pltpu.VMEM((2, SLOTS_E, D), BF16),
        pltpu.VMEM((SLOTS, D), BF16),
        pltpu.VMEM((SLOTS, D), BF16),
        pltpu.VMEM((FF, D), BF16),
        pltpu.VMEM((FF, D), BF16),
        pltpu.VMEM((FF, FF), F32),
        pltpu.VMEM((FF, FF), BF16),
        pltpu.VMEM((FF, FF), BF16),
        pltpu.VMEM((128, D), BF16),
        pltpu.VMEM((2, 32, D), BF16),
        sem((NE,)),
        sem((NE,)),
        sem((2, 4, 2)),
        sem((2, 4, 2)),
        sem((8, 2)),
        sem((8, 2)),
        sem((2,)),
        sem((NX,)),
        sem((2, 4, 2)),
        sem((2, 4, 2)),
        sem((2, 2)),
        sem((NX, 2)),
        sem((2, 4)),
        sem((NX, 4)),
        sem((NX, 4)),
        sem((2, 4)),
        sem((2,)),
        sem((2,)),
        sem((2,)),
        sem((2,)),
        sem((2,)),
        sem((2,)),
        sem((2,)),
        sem((2,)),
        sem((2, 4, 4)),
        sem((2, 4, 4)),
        sem((NY,)),
        sem((NY,)),
        sem((NX,)),
        sem((2,)),
        pltpu.VMEM((2 * TOK, SLOTS), BF16),
        pltpu.VMEM((TOK, D), F32),
        pltpu.VMEM((TOK, D), F32),
        sem,
        sem,
    ]
    return pl.pallas_call(
        kernel,
        out_shape=(
            jax.ShapeDtypeStruct((TOK, D), BF16),
            jax.ShapeDtypeStruct((ROWS, 2, D), F32),
        ),
        in_specs=[anywhere] * 6 + [pl.BlockSpec(memory_space=pltpu.SMEM), anywhere],
        out_specs=(vmem, vmem),
        scratch_shapes=scratch,
        compiler_params=pltpu.CompilerParams(
            collective_id=0, has_side_effects=True, vmem_limit_bytes=60 * 2**20
        ),
        cost_estimate=pl.CostEstimate(
            flops=16 * 10**9, bytes_accessed=5 * 10**6, transcendentals=450560
        ),
        name="expert_backward",
    )(tokens, weights, gate, adjoint, chosen.T, seat.T, quota, jnp.asarray(layout_tables()))


def solution(mesh):
    return jax.shard_map(
        body,
        mesh=mesh,
        in_specs=(
            P(("dp", "expert"), None),
            P("dp", "expert", None),
            P(None, ("dp", "expert")),
            P(None, ("dp", "expert")),
            P(("dp", "expert"), None),
            P(("dp", "expert"), None),
            P(),
        ),
        out_specs=(P(("dp", "expert"), None), P("dp", "expert", None)),
        check_vma=False,
    )
```

```python
import math

import jax
import jax.numpy as jnp
import numpy as np
from jax import lax
from jax.experimental import pallas as pl
from jax.experimental.pallas import tpu as pltpu
from jax.sharding import PartitionSpec as P

MESH = pl.DeviceIdType.MESH
F32 = jnp.float32
BF16 = jnp.bfloat16

ITERS = 2
QUINT_A = 3.4445
QUINT_B = -4.775
QUINT_C = 2.0315
EPSILON = 1e-06

NX, NY, NZ = 4, 8, 8
NE = 2 * NY
FF, D = 704, 1024
TOK, TOP = 128, 6
CAP = 20
SLOTS = 2 * NE * CAP
ROWS = FF // (NX * NZ)
WPAD = 32
GROUP = 4 * CAP
SLOTS_E = NE * CAP
S_PARTS = ((0, 80), (80, 80), (160, 80), (240, 32), (272, 48))
DEPTH = 384
ZROWS = NX * ROWS
ZBLK = 96
ZPIECES = ((0, 48), (48, 48))
REL = (0, -1, 1, -2, 2, -3, 3, 4)
HALF = FF // 2
PART = FF // 4
PIECE = TOK // 2

UP, DOWN = 0, 1


def layout_tables():
    table = np.full((8, DEPTH), -1, np.int32)
    table[1, :] = -(1 << 20)
    for n in range(NY):
        for core in range(2):
            for p in range(CAP):
                at = (n * 2 + core) * CAP + p
                table[0, at] = REL[n] % NY
                table[1, at] = core * 2 * CAP + p
    for k in range(NX):
        for i in range(ROWS):
            table[2, k * WPAD + i] = k * ROWS + i
    return table


def dot(a, b):
    return jnp.dot(a, b, preferred_element_type=F32)


def dot_nt(a, b):
    return lax.dot_general(a, b, (((1,), (1,)), ((), ())), preferred_element_type=F32)


def kernel(
    tok_hbm,
    w_hbm,
    gate_hbm,
    adj_hbm,
    chosen_hbm,
    seat_hbm,
    quota_ref,
    lay_hbm,
    out_tok,
    out_rows,
    w_ref,
    gate_ref,
    adj_ref,
    chosen_ref,
    seat_ref,
    lay_ref,
    in_s,
    tokv,
    wsend,
    wx,
    wst,
    tbl,
    u_ref,
    uown,
    utail,
    utails,
    ucat,
    ut,
    wnat,
    sown,
    scat,
    zsend,
    zown,
    near,
    third,
    fourth,
    far,
    sg,
    sgl,
    sgo,
    ret,
    grad,
    x1_ref,
    gram_sum,
    gram,
    poly,
    rows_ref,
    fin,
    t_s,
    t_r,
    y_s,
    y_r,
    c_s,
    c_r,
    w_s,
    w_r,
    z_s,
    z_r,
    uc_s,
    uc_r,
    sc_s,
    sc_r,
    sg_s,
    sg_r,
    nr_s,
    nr_r,
    th_s,
    th_r,
    fo_s,
    fo_r,
    fr_s,
    fr_r,
    ag_s,
    ag_r,
    rt_s,
    rt_r,
    fn_s,
    fn_r,
    picked,
    for_sibling,
    from_sibling,
    sib_s,
    sib_r,
):
    dp = lax.axis_index("dp")
    me = lax.axis_index("expert")
    x, z = lax.rem(dp, NX), dp // NX
    y, c = me // 2, lax.rem(me, 2)

    def wrap(v, n):
        return lax.rem(v + 2 * n, n)

    def peer(dx=0, dy=0, dz=0, dc=0):
        core = lax.rem(c + dc, 2)
        return (wrap(z + dz, NZ) * NX + wrap(x + dx, NX), wrap(y + dy, NY) * 2 + core)

    def copy(ref_src, ref_dst, ssem, rsem, device):
        return pltpu.make_async_remote_copy(
            src_ref=ref_src,
            dst_ref=ref_dst,
            send_sem=ssem,
            recv_sem=rsem,
            device_id=device,
            device_id_type=MESH,
        )

    def aligned(v, m):
        return pl.multiple_of(v, m)

    barrier = pltpu.get_barrier_semaphore()
    greeted = [(dp, lax.rem(me + i, NE)) for i in range(1, NE)]
    greeted += [peer(dz=k) for k in (-2, -1, 1, 2)]
    greeted += [peer(dx=k) for k in range(1, NX)]
    for device in greeted:
        pl.semaphore_signal(barrier, inc=1, device_id=device, device_id_type=MESH)

    own_rows = pl.ds(aligned(y * (2 * TOK) + c * TOK, TOK), TOK)
    operands = (
        (tok_hbm, tokv.at[own_rows, :]),
        (w_hbm, w_ref),
        (chosen_hbm, chosen_ref),
        (seat_hbm, seat_ref),
        (lay_hbm, lay_ref),
        (gate_hbm, gate_ref),
        (adj_hbm, adj_ref),
    )
    loads = [pltpu.make_async_copy(a, b, in_s.at[i]) for i, (a, b) in enumerate(operands)]
    for cp in loads:
        cp.start()
    for cp in loads[:4]:
        cp.wait()

    chosen = chosen_ref[...]
    quota = jnp.zeros_like(chosen)
    for e in range(2 * NE):
        quota = jnp.where(chosen == e, quota_ref[e], quota)
    code = jnp.where(seat_ref[...] < quota, chosen * 32 + seat_ref[...], -1)
    tbl[me, 0:TOP, :] = code
    tbl[me, TOP:8, :] = jnp.full((8 - TOP, TOK), -1, jnp.int32)

    def tok_rows(yb, cb, p):
        return pl.ds(aligned(yb * (2 * TOK) + cb * TOK + p * PIECE, PIECE), PIECE)

    def wx_rows(xb):
        return pl.ds(aligned(xb * WPAD, WPAD), WPAD)

    blank = jnp.zeros((WPAD - ROWS, D), BF16)
    for l in range(2):
        wsend[l] = jnp.concatenate([w_ref[:, l, :], blank], axis=0)
    for k in range(NX):
        scat[k * DEPTH + SLOTS_E : (k + 1) * DEPTH, :] = jnp.zeros((DEPTH - SLOTS_E, D), BF16)

    r0 = wrap(x - 2 * c, NX)
    is_owner = r0 < 2
    l_own = lax.rem(r0, 2)

    pl.semaphore_wait(barrier, len(greeted))

    sent = []

    def start(cp):
        cp.start()
        sent.append(cp)

    def drain():
        for cp in sent:
            cp.wait_send()
        sent.clear()

    def y_copy(direction, hop, p):
        step = 1 if direction == UP else -1
        yb = wrap(y - step * (hop - 1), NY)
        view = tokv.at[tok_rows(yb, c, p), :]
        at = (direction, hop - 1, p)
        return copy(view, view, y_s.at[at], y_r.at[at], peer(dy=step))

    def y_arrival(direction, hop, p):
        step = 1 if direction == UP else -1
        yb = wrap(y - step * hop, NY)
        view = tokv.at[tok_rows(yb, c, p), :]
        at = (direction, hop - 1, p)
        return yb, copy(view, view, y_s.at[at], y_r.at[at], peer(dy=step))

    def to_sibling(n, p):
        yb = wrap(y + REL[n], NY)
        view = tokv.at[tok_rows(yb, c, p), :]
        start(copy(view, view, c_s.at[n, p], c_r.at[n, p], peer(dc=1)))

    def y_recv(direction, hop, p):
        _, cp = y_arrival(direction, hop, p)
        cp.wait_recv()
        if hop < 3 or (hop == 3 and p == direction):
            start(y_copy(direction, hop + 1, p))
        step = 1 if direction == UP else -1
        n = REL.index(-step * hop) if hop < 4 else 7
        to_sibling(n, p)

    def to_owner(l, make):
        k = wrap(x - 2 * c - l, NX)

        @pl.when(k != 0)
        def _():
            make(k, ((z * NX + 2 * c + l), me)).start()

    def w_copy(l):
        def make(k, device):
            return copy(wsend.at[l], wx.at[wx_rows(x), :], w_s.at[l], w_r.at[k], device)

        return make

    def x_weights():
        for l in range(2):
            to_owner(l, w_copy(l))

    def x_weights_recv():
        wx[wx_rows(x), :] = wsend[l_own]
        for k in range(1, NX):
            view = wx.at[wx_rows(wrap(x + k, NX)), :]
            copy(view, view, w_s.at[0], w_r.at[k], peer(dx=k)).wait_recv()
        pick = jnp.where(
            lax.broadcasted_iota(jnp.int32, (ZBLK, NX * WPAD), 0) == lay_ref[2:3, 0 : NX * WPAD],
            1.0,
            0.0,
        ).astype(BF16)
        wst[pl.ds(aligned(z * ZBLK, 16), ZBLK), :] = dot(pick, wx[...]).astype(BF16)
        for p in range(2):
            for direction in (UP, DOWN):
                z_copy(direction, 1, p).start()

    def z_view(zb, p):
        first, count = ZPIECES[p]
        return wst.at[pl.ds(aligned(zb * ZBLK + first, 16), count), :]

    def z_copy(direction, hop, p):
        step = 1 if direction == UP else -1
        view = z_view(wrap(z - step * (hop - 1), NZ), p)
        at = (direction, hop - 1, p)
        return copy(view, view, z_s.at[at], z_r.at[at], peer(dz=step))

    def z_recv(direction, hop, p):
        step = 1 if direction == UP else -1
        view = z_view(wrap(z - step * hop, NZ), p)
        at = (direction, hop - 1, p)
        copy(view, view, z_s.at[at], z_r.at[at], peer(dz=step)).wait_recv()
        if hop < 3 or (hop == 3 and p == direction):
            z_copy(direction, hop + 1, p).start()

    def z_both(hop, p):
        z_recv(UP, hop, p)
        z_recv(DOWN, hop, p)

    def up_grad(t):
        def tile(i, carry):
            rows = pl.ds(aligned(t * HALF + i * 32, 32), 32)
            g = gate_ref[rows, :].astype(F32)
            a = adj_ref[rows, :].astype(F32)
            u_ref[rows, :] = (a * (g / (1.0 + jnp.exp(-g)))).astype(BF16)
            return carry

        lax.fori_loop(0, HALF // 32, tile, 0)

    def u_copy(l, t):
        rows = pl.ds(t * HALF, HALF)

        def make(k, device):
            return copy(
                uown.at[l, rows, pl.ds(0, 256)],
                ucat.at[rows, pl.ds(aligned(k * DEPTH, DEPTH), 256)],
                uc_s.at[l, t],
                uc_r.at[k, t],
                device,
            )

        return make

    def u_tail_copy(l):
        def make(k, device):
            return copy(utail.at[l], utails.at[k], uc_s.at[l, 2], uc_r.at[k, 2], device)

        return make

    def unpack(k):
        lane = lax.broadcasted_iota(jnp.int32, (HALF, 128), 1)
        both = utails[k].astype(F32)
        for t in range(2):
            moved = both if t == 0 else jnp.concatenate([both[:, 64:], both[:, :64]], axis=1)
            ucat[t * HALF : (t + 1) * HALF, k * DEPTH + 256 : (k + 1) * DEPTH] = jnp.where(
                lane < 64, moved, 0.0
            ).astype(BF16)

    def s_copy(l, g):
        first, count = S_PARTS[g]

        def make(k, device):
            return copy(
                sown.at[l, pl.ds(first, count), :],
                scat.at[pl.ds(aligned(k * DEPTH + first, 16), count), :],
                sc_s.at[l, g],
                sc_r.at[k, g],
                device,
            )

        return make

    def expert_major():
        chip = jnp.bitwise_and(lay_ref[0:1, 0:DEPTH] + y, NY - 1)
        tails = [[], []]
        for t in range(2):
            rows = slice(t * HALF, (t + 1) * HALF)
            up_grad(t)
            for l in range(2):
                source = chip * (4 * CAP) + lay_ref[1:2, 0:DEPTH] + l * CAP
                pick = jnp.where(
                    lax.broadcasted_iota(jnp.int32, (SLOTS, DEPTH), 0) == source, 1.0, 0.0
                ).astype(BF16)
                full = dot(u_ref[rows, :], pick)
                uown[l, rows, :] = full.astype(BF16)
                tails[l].append(full[:, 256 : 256 + 64])
                to_owner(l, u_copy(l, t))
        for l in range(2):
            utail[l] = jnp.concatenate(tails[l], axis=1).astype(BF16)
            to_owner(l, u_tail_copy(l))

    def u_recv():
        ucat[:, 0:DEPTH] = uown[l_own]
        for k in range(1, NX):
            for t in range(2):
                view = ucat.at[pl.ds(t * HALF, HALF), pl.ds(k * DEPTH, 256)]
                copy(view, view, uc_s.at[0, t], uc_r.at[k, t], peer(dx=k)).wait_recv()
            view = utails.at[k]
            copy(view, view, uc_s.at[0, 2], uc_r.at[k, 2], peer(dx=k)).wait_recv()
            unpack(k)

    def transposed(k):
        row = lax.broadcasted_iota(jnp.int32, (SLOTS_E, DEPTH), 0)
        col = lax.broadcasted_iota(jnp.int32, (SLOTS_E, DEPTH), 1)
        same = jnp.where(row == col, 1.0, 0.0).astype(BF16)
        ut[k * SLOTS_E : (k + 1) * SLOTS_E, :] = dot_nt(
            same, ucat[:, k * DEPTH : (k + 1) * DEPTH]
        ).astype(BF16)

    def slot_grads():
        for zb in range(NZ):
            wnat[zb * ZROWS : (zb + 1) * ZROWS, :] = wst[zb * ZBLK : zb * ZBLK + ZROWS, :]
        for n in range(4):
            cols = slice(n * 256, (n + 1) * 256)
            sg[:, cols] = dot(ut[...], wnat[:, cols]).astype(BF16)

    def sg_copy(k, g):
        return copy(
            sg.at[pl.ds(k * SLOTS_E + g * GROUP, GROUP), :],
            sgl.at[l_own, pl.ds(g * GROUP, GROUP), :],
            sg_s.at[k, g],
            sg_r.at[l_own, g],
            peer(dx=k),
        )

    def gather_chip(n):
        yb = wrap(y + REL[n], NY)
        for p in range(2):
            view = tokv.at[tok_rows(yb, 1 - c, p), :]
            copy(view, view, c_s.at[n, p], c_r.at[n, p], peer(dc=1)).wait_recv()
        far = 1 << 12
        codes = jnp.concatenate([tbl[yb * 2], tbl[yb * 2 + 1] + far], axis=1)
        row = lax.broadcasted_iota(jnp.int32, (GROUP, 2 * TOK), 0)
        want = row
        for b in range(1, 4):
            want = jnp.where(row >= b * CAP, row + (b % 2) * far + (b // 2) * 32 - b * CAP, want)
        want = want + (2 * me) * 32
        hit = jnp.zeros((GROUP, 2 * TOK), F32)
        for k in range(TOP):
            hit = hit + jnp.where(codes[k : k + 1, :] == want, 1.0, 0.0)
        tokens = tokv[pl.ds(aligned(yb * 2 * TOK, 2 * TOK), 2 * TOK), :]
        return dot(hit.astype(BF16), tokens)

    def place(g, values):
        first, count = S_PARTS[g]
        rows = slice(first, first + count)
        for l in range(2):
            sown[l, rows, :] = values[l].astype(BF16)
            to_owner(l, s_copy(l, g))

        @pl.when(is_owner)
        def _():
            scat[rows, :] = sown[l_own, rows, :]

    def gather(g):
        two = [gather_chip(n) for n in (2 * g, 2 * g + 1)]
        per = 2 * CAP
        place(g, [jnp.concatenate([v[l * per : (l + 1) * per] for v in two]) for l in range(2)])

    for p in range(2):
        for direction in (UP, DOWN):
            start(y_copy(direction, 1, p))
    x_weights()
    for i in range(1, NE):
        j = lax.rem(me + i, NE)
        start(copy(tbl.at[me], tbl.at[me], t_s.at[i], t_r.at[i], (dp, j)))
    for p in range(2):
        to_sibling(0, p)

    def y_both(hop, p):
        y_recv(UP, hop, p)
        y_recv(DOWN, hop, p)

    for cp in loads[4:]:
        cp.wait()
    expert_major()
    y_both(1, 0)

    @pl.when(is_owner)
    def _():
        x_weights_recv()

    y_both(1, 1)
    for i in range(1, NE):
        j = lax.rem(me + NE - i, NE)
        copy(tbl.at[j], tbl.at[j], t_s.at[i], t_r.at[i], (dp, j)).wait_recv()
    gather(0)

    @pl.when(is_owner)
    def _():
        z_both(1, 0)
        z_both(1, 1)

    y_both(2, 0)

    @pl.when(is_owner)
    def _():
        z_both(2, 0)
        z_both(2, 1)

    y_both(2, 1)
    gather(1)

    @pl.when(is_owner)
    def _():
        z_both(3, 0)
        z_both(3, 1)

    y_both(3, 0)

    @pl.when(is_owner)
    def _():
        u_recv()
        transposed(0)
        transposed(1)

    y_both(3, 1)
    gather(2)
    sixth = gather_chip(6)
    place(3, [sixth[0:32], sixth[40:72]])

    @pl.when(is_owner)
    def _():
        transposed(2)
        transposed(3)
        z_recv(UP, 4, 0)
        z_recv(DOWN, 4, 1)

    y_recv(UP, 4, 0)
    y_recv(DOWN, 4, 1)
    seventh = gather_chip(7)
    place(4, [jnp.concatenate([sixth[32:40], seventh[0:40]]), jnp.concatenate([sixth[72:80], seventh[40:80]])])

    @pl.when(is_owner)
    def _():
        slot_grads()
        for g in (3, 2, 1, 0):
            for k in range(1, NX):
                sg_copy(k, g).start()
        sgl[l_own] = sg[0:SLOTS_E, :]

    z2 = z // 2
    odd = lax.rem(z, 2)
    order = [wrap(z2 + k, 4) for k in (2, 1 + 2 * odd, 3 - 2 * odd, 0)]

    def cols2(i):
        return pl.ds(aligned(order[i] * 256, 256), 256)

    def zchunk(r):
        return pl.ds(aligned(wrap(z + r, NZ) * 128, 128), 128)

    def direct_copy(d):
        r, step = ((1, 1), (7, -1))[d]
        return copy(zsend.at[:, zchunk(r)], near.at[d], nr_s.at[d], nr_r.at[d], peer(dz=step))

    def third_copy(d):
        r, step = ((3, 1), (5, -1))[d]
        return copy(zsend.at[:, zchunk(r)], third.at[d], th_s.at[d], th_r.at[d], peer(dz=step))

    def fourth_copy(d):
        step = (2, -2)[d]
        rows = pl.ds(d * HALF, HALF)
        return copy(
            zsend.at[rows, zchunk(4)], fourth.at[d], fo_s.at[d], fo_r.at[d], peer(dz=step)
        )

    def relayed_copy(d):
        r, step = ((2, 2), (6, -2))[d]
        return copy(zsend.at[:, zchunk(r)], far.at[d], fr_s.at[d], fr_r.at[d], peer(dz=step))

    def relay(d):
        r = (2, 6)[d]
        third_copy(d).wait_recv()
        fourth_copy(d).wait_recv()
        for t in range(2):
            rows = slice(t * HALF, (t + 1) * HALF)
            total = zsend[rows, zchunk(r)].astype(F32) + third[d, rows, :].astype(F32)
            if t == d:
                total = total + fourth[d].astype(F32)
            zsend[rows, zchunk(r)] = total.astype(BF16)
        relayed_copy(d).start()

    @pl.when(is_owner)
    def _():
        for g in range(5):
            for k in range(1, NX):
                view = scat.at[pl.ds(k * DEPTH + S_PARTS[g][0], S_PARTS[g][1]), :]
                copy(view, view, sc_s.at[0, 0], sc_r.at[k, g], peer(dx=k)).wait_recv()
        for i in range(4):
            halves = []
            for t in range(2):
                rows = slice(t * HALF, (t + 1) * HALF)
                halves.append(dot(ucat[rows, :], scat[:, cols2(i)]))
                zsend[rows, cols2(i)] = halves[t].astype(BF16)
            for parity in range(2):

                @pl.when(odd == parity)
                def _():
                    if i == 0:
                        fourth_copy(0).start()
                        fourth_copy(1).start()
                        third_copy(1 - parity).start()
                    elif i == 1:
                        third_copy(parity).start()
                    elif i == 2:
                        direct_copy(1 - parity).start()
                    else:
                        direct_copy(parity).start()
                        first = parity * 128
                        for t in range(2):
                            rows = slice(t * HALF, (t + 1) * HALF)
                            zown[rows, :] = halves[t][:, first : first + 128]

    def chip_rows(yb):
        return pl.ds(aligned(yb * GROUP, 16), GROUP)

    def return_copy(n):
        yb = wrap(y + REL[n], NY)
        return copy(
            sgo.at[pl.ds(n * GROUP, GROUP), :],
            ret.at[chip_rows(y), :],
            rt_s.at[n],
            rt_r.at[n],
            (dp, yb * 2 + c),
        )

    def send_back(g):
        for l in range(2):

            @pl.when(x != 2 * c + l)
            def _():
                view = sgl.at[l, pl.ds(g * GROUP, GROUP), :]
                copy(view, view, sg_s.at[1, g], sg_r.at[l, g], peer(dx=1)).wait_recv()

        for n in (2 * g + 1, 2 * g):
            both = [sgl[l, n * 2 * CAP : (n + 1) * 2 * CAP, :] for l in range(2)]
            sgo[n * GROUP : (n + 1) * GROUP, :] = jnp.concatenate(both, axis=0)
            if n:
                start(return_copy(n))


    drain()
    for l in range(2):
        k = wrap(x - 2 * c - l, NX)

        @pl.when(k != 0)
        def _():
            device = (z * NX + 2 * c + l, me)
            w_copy(l)(k, device).wait_send()
            u_copy(l, 0)(k, device).wait_send()
            u_copy(l, 1)(k, device).wait_send()
            u_tail_copy(l)(k, device).wait_send()
            for g in range(5):
                s_copy(l, g)(k, device).wait_send()

    send_back(3)
    send_back(2)

    @pl.when(is_owner)
    def _():
        relay(0)
        relay(1)

    @pl.when(is_owner)
    def _():
        for hop in range(1, 5):
            for p in range(2):
                for direction in (UP, DOWN):
                    if hop < 4 or p == direction:
                        z_copy(direction, hop, p).wait_send()

    send_back(1)
    send_back(0)
    ret[chip_rows(y), :] = sgo[0:GROUP, :]

    codes = jnp.concatenate([tbl[2 * y], tbl[2 * y + 1] + (1 << 12)], axis=1)
    row = lax.broadcasted_iota(jnp.int32, (GROUP, 2 * TOK), 0)
    want = row
    for b in range(1, 4):
        want = jnp.where(row >= b * CAP, row + (b % 2) * (1 << 12) + (b // 2) * 32 - b * CAP, want)
    picks = []
    for yb in range(NY):
        base = want + (yb * 4 + 2 * c) * 32
        hit = jnp.zeros((GROUP, 2 * TOK), F32)
        for k in range(TOP):
            hit = hit + jnp.where(codes[k : k + 1, :] == base, 1.0, 0.0)
        picks.append(hit)
    picked[...] = jnp.concatenate(picks, axis=0).T.astype(BF16)

    zcols = pl.ds(aligned(z * 128, 128), 128)

    def ag_view(zb, p):
        return grad.at[pl.ds(p * PART, PART), pl.ds(aligned(zb * 128, 128), 128)]

    def ag_copy(direction, hop, p):
        step = 1 if direction == UP else -1
        view = ag_view(wrap(z - step * (hop - 1), NZ), p)
        at = (direction, hop - 1, p)
        return copy(view, view, ag_s.at[at], ag_r.at[at], peer(dz=step))

    def ag_recv(direction, hop, p):
        step = 1 if direction == UP else -1
        view = ag_view(wrap(z - step * hop, NZ), p)
        at = (direction, hop - 1, p)
        copy(view, view, ag_s.at[at], ag_r.at[at], peer(dz=step)).wait_recv()
        if hop < 3 or (hop == 3 and p // 2 == direction):
            ag_copy(direction, hop + 1, p).start()

    def rows_copy(k):
        xd = wrap(x + k, NX)
        return copy(
            rows_ref.at[pl.ds(aligned(xd * 32, 32), 32), :],
            fin.at[l_own],
            fn_s.at[k],
            fn_r.at[l_own],
            peer(dx=k),
        )

    @pl.when(is_owner)
    def _():
        total = zown[...]
        for d in range(2):
            direct_copy(d).wait_recv()
            total = total + near[d].astype(F32)
        for d in range(2):
            relayed_copy(d).wait_recv()
            total = total + far[d].astype(F32)
        grad[:, zcols] = total.astype(BF16)
        for p in range(4):
            for direction in (UP, DOWN):
                ag_copy(direction, 1, p).start()
        squares = jnp.zeros((1, 256), F32)
        for hop in range(1, 5):
            if hop < 4:
                for p in range(4):
                    for direction in (UP, DOWN):
                        ag_recv(direction, hop, p)
                pair = (z - hop, z + hop)
            else:
                for p in range(2):
                    ag_recv(UP, 4, p)
                    ag_recv(DOWN, 4, 2 + p)
                pair = (z + 4, z)
            both = jnp.concatenate(
                [grad[:, pl.ds(aligned(wrap(zb, NZ) * 128, 128), 128)] for zb in pair], axis=1
            )
            wide = both.astype(F32)
            squares = squares + jnp.sum(wide * wide, axis=0, keepdims=True)
            for t in range(2):
                rows = slice(t * HALF, (t + 1) * HALF)
                term = dot_nt(both[rows, :], both)
                if hop > 1:
                    term = gram_sum[rows, :] + term
                if hop < 4:
                    gram_sum[rows, :] = term
                else:
                    norm = jnp.sqrt(jnp.sum(squares, axis=1, keepdims=True))
                    inverse = 1.0 / (norm + EPSILON)
                    gram[rows, :] = (term * inverse * inverse).astype(BF16)

        halves = [slice(0, HALF), slice(HALF, FF)]
        for rows in halves:
            square = dot(gram[rows, :], gram[...])
            poly[rows, :] = (QUINT_B * gram[rows, :].astype(F32) + QUINT_C * square).astype(BF16)
        for rows in halves:
            x1_ref[rows, :] = (
                inverse * (QUINT_A * grad[rows, :].astype(F32) + dot(poly[rows, :], grad[...]))
            ).astype(BF16)
        for rows in halves:
            gram[rows, :] = dot_nt(x1_ref[rows, :], x1_ref[...]).astype(BF16)
        picks = []
        for xd in range(NX):
            r = lax.broadcasted_iota(jnp.int32, (32, FF), 0)
            f = lax.broadcasted_iota(jnp.int32, (32, FF), 1)
            hit = jnp.logical_and(r < ROWS, f == r + (z * NX + xd) * ROWS)
            picks.append(jnp.where(hit, 1.0, 0.0))
        pick = jnp.concatenate(picks, axis=0).astype(BF16)
        gram_rows = dot(pick, gram[...]).astype(BF16)
        it_rows = dot(pick, x1_ref[...])
        poly_rows = (QUINT_B * gram_rows.astype(F32) + QUINT_C * dot(gram_rows, gram[...])).astype(
            BF16
        )
        rows_ref[...] = (QUINT_A * it_rows + dot(poly_rows, x1_ref[...])).astype(BF16)
        for k in range(1, NX):
            rows_copy(k).start()
        for d in range(2):
            direct_copy(d).wait_send()
            third_copy(d).wait_send()
            fourth_copy(d).wait_send()
            relayed_copy(d).wait_send()
        for hop in range(1, 5):
            for p in range(4):
                for direction in (UP, DOWN):
                    if hop < 4 or p // 2 == direction:
                        ag_copy(direction, hop, p).wait_send()
        for g in range(4):
            for k in range(1, NX):
                sg_copy(k, g).wait_send()
        fin[l_own] = rows_ref[pl.ds(aligned(x * 32, 32), 32), :]

    for n in range(1, NY):
        view = ret.at[chip_rows(wrap(y - REL[n], NY)), :]
        copy(view, view, rt_s.at[n], rt_r.at[n], peer(dy=-REL[n])).wait_recv()

    def core_rows(core):
        return pl.ds(aligned(core * TOK, TOK), TOK)

    for_sibling[...] = dot(picked[core_rows(1 - c), :], ret[...])
    sibling = copy(for_sibling, from_sibling, sib_s, sib_r, peer(dc=1))
    start(sibling)
    mine = dot(picked[core_rows(c), :], ret[...])
    sibling.wait_recv()
    out_tok[...] = (mine + from_sibling[...]).astype(BF16)

    for l in range(2):
        owner_x = 2 * c + l

        @pl.when(x != owner_x)
        def _():
            view = fin.at[l]
            copy(view, view, fn_s.at[1], fn_r.at[l], peer(dx=1)).wait_recv()

        out_rows[l] = fin[l]

    drain()

    @pl.when(is_owner)
    def _():
        for k in range(1, NX):
            rows_copy(k).wait_send()


def results(token_ref, rows_ref, out_tok, out_mu):
    scale = 0.2 * math.sqrt(max(FF, D))
    out_tok[...] = token_ref[...]
    for l in range(2):
        out_mu[:, l, :] = scale * rows_ref[l, 0:ROWS, :].astype(F32)


def body(tokens, weights, gate, adjoint, chosen, seat, quota):
    vmem = pl.BlockSpec(memory_space=pltpu.VMEM)
    anywhere = pl.BlockSpec(memory_space=pl.ANY)
    sem = pltpu.SemaphoreType.DMA
    scratch = [
        pltpu.VMEM((ROWS, 2, D), BF16),
        pltpu.VMEM((FF, SLOTS), BF16),
        pltpu.VMEM((FF, SLOTS), BF16),
        pltpu.VMEM((TOP, TOK), jnp.int32),
        pltpu.VMEM((TOP, TOK), jnp.int32),
        pltpu.VMEM((8, DEPTH), jnp.int32),
        sem((7,)),
        pltpu.VMEM((NE * TOK, D), BF16),
        pltpu.VMEM((2, WPAD, D), BF16),
        pltpu.VMEM((NX * WPAD, D), BF16),
        pltpu.VMEM((NZ * ZBLK, D), BF16),
        pltpu.VMEM((NE, 8, TOK), jnp.int32),
        pltpu.VMEM((FF, SLOTS), BF16),
        pltpu.VMEM((2, FF, DEPTH), BF16),
        pltpu.VMEM((2, HALF, 128), BF16),
        pltpu.VMEM((NX, HALF, 128), BF16),
        pltpu.VMEM((FF, NX * DEPTH), BF16),
        pltpu.VMEM((NX * SLOTS_E, FF), BF16),
        pltpu.VMEM((FF, D), BF16),
        pltpu.VMEM((2, SLOTS_E, D), BF16),
        pltpu.VMEM((NX * DEPTH, D), BF16),
        pltpu.VMEM((FF, D), BF16),
        pltpu.VMEM((FF, 128), F32),
        pltpu.VMEM((2, FF, 128), BF16),
        pltpu.VMEM((2, FF, 128), BF16),
        pltpu.VMEM((2, HALF, 128), BF16),
        pltpu.VMEM((2, FF, 128), BF16),
        pltpu.VMEM((NX * SLOTS_E, D), BF16),
        pltpu.VMEM((2, SLOTS_E, D), BF16),
        pltpu.VMEM((SLOTS, D), BF16),
        pltpu.VMEM((SLOTS, D), BF16),
        pltpu.VMEM((FF, D), BF16),
        pltpu.VMEM((FF, D), BF16),
        pltpu.VMEM((FF, FF), F32),
        pltpu.VMEM((FF, FF), BF16),
        pltpu.VMEM((FF, FF), BF16),
        pltpu.VMEM((128, D), BF16),
        pltpu.VMEM((2, 32, D), BF16),
        sem((NE,)),
        sem((NE,)),
        sem((2, 4, 2)),
        sem((2, 4, 2)),
        sem((8, 2)),
        sem((8, 2)),
        sem((2,)),
        sem((NX,)),
        sem((2, 4, 2)),
        sem((2, 4, 2)),
        sem((2, 3)),
        sem((NX, 3)),
        sem((2, 5)),
        sem((NX, 5)),
        sem((NX, 4)),
        sem((2, 4)),
        sem((2,)),
        sem((2,)),
        sem((2,)),
        sem((2,)),
        sem((2,)),
        sem((2,)),
        sem((2,)),
        sem((2,)),
        sem((2, 4, 4)),
        sem((2, 4, 4)),
        sem((NY,)),
        sem((NY,)),
        sem((NX,)),
        sem((2,)),
        pltpu.VMEM((2 * TOK, SLOTS), BF16),
        pltpu.VMEM((TOK, D), F32),
        pltpu.VMEM((TOK, D), F32),
        sem,
        sem,
    ]
    token_grad, update_rows = pl.pallas_call(
        kernel,
        out_shape=(
            jax.ShapeDtypeStruct((TOK, D), BF16),
            jax.ShapeDtypeStruct((2, 32, D), BF16),
        ),
        in_specs=[anywhere] * 6 + [pl.BlockSpec(memory_space=pltpu.SMEM), anywhere],
        out_specs=(vmem, vmem),
        scratch_shapes=scratch,
        compiler_params=pltpu.CompilerParams(
            collective_id=0, has_side_effects=True, vmem_limit_bytes=60 * 2**20
        ),
        cost_estimate=pl.CostEstimate(
            flops=16 * 10**9, bytes_accessed=5 * 10**6, transcendentals=450560
        ),
        name="expert_backward",
    )(tokens, weights, gate, adjoint, chosen.T, seat.T, quota, jnp.asarray(layout_tables()))
    return pl.pallas_call(
        results,
        out_shape=(
            jax.ShapeDtypeStruct((TOK, D), BF16),
            jax.ShapeDtypeStruct((ROWS, 2, D), F32),
        ),
        in_specs=[vmem] * 2,
        out_specs=(vmem, vmem),
        cost_estimate=pl.CostEstimate(flops=45056, bytes_accessed=10**6, transcendentals=0),
        name="results",
    )(token_grad, update_rows)


def solution(mesh):
    return jax.shard_map(
        body,
        mesh=mesh,
        in_specs=(
            P(("dp", "expert"), None),
            P("dp", "expert", None),
            P(None, ("dp", "expert")),
            P(None, ("dp", "expert")),
            P(("dp", "expert"), None),
            P(("dp", "expert"), None),
            P(),
        ),
        out_specs=(P(("dp", "expert"), None), P("dp", "expert", None)),
        check_vma=False,
    )
```

```python
import math

import jax
import jax.numpy as jnp
import numpy as np
from jax import lax
from jax.experimental import pallas as pl
from jax.experimental.pallas import tpu as pltpu
from jax.sharding import PartitionSpec as P

MESH = pl.DeviceIdType.MESH
F32 = jnp.float32
BF16 = jnp.bfloat16

ITERS = 2
QUINT_A = 3.4445
QUINT_B = -4.775
QUINT_C = 2.0315
EPSILON = 1e-06

NX, NY, NZ = 4, 8, 8
NE = 2 * NY
FF, D = 704, 1024
TOK, TOP = 128, 6
CAP = 20
SLOTS = 2 * NE * CAP
ROWS = FF // (NX * NZ)
WPAD = 32
GROUP = 4 * CAP
SLOTS_E = NE * CAP
S_PARTS = ((0, 80), (80, 80), (160, 80), (240, 32), (272, 48))
DEPTH = 384
ZROWS = NX * ROWS
ZBLK = 96
ZPIECES = ((0, 48), (48, 48))
REL = (0, -1, 1, -2, 2, -3, 3, 4)
HALF = FF // 2
PART = FF // 4
PIECE = TOK // 2

UP, DOWN = 0, 1


def layout_tables():
    table = np.full((8, DEPTH), -1, np.int32)
    table[1, :] = -(1 << 20)
    for n in range(NY):
        for core in range(2):
            for p in range(CAP):
                at = (n * 2 + core) * CAP + p
                table[0, at] = REL[n] % NY
                table[1, at] = core * 2 * CAP + p
    for k in range(NX):
        for i in range(ROWS):
            table[2, k * WPAD + i] = k * ROWS + i
    return table


def dot(a, b):
    return jnp.dot(a, b, preferred_element_type=F32)


def dot_nt(a, b):
    return lax.dot_general(a, b, (((1,), (1,)), ((), ())), preferred_element_type=F32)


def kernel(
    tok_hbm,
    w_hbm,
    gate_hbm,
    adj_hbm,
    chosen_hbm,
    seat_hbm,
    quota_ref,
    lay_hbm,
    out_tok,
    out_rows,
    w_ref,
    gate_ref,
    adj_ref,
    chosen_ref,
    seat_ref,
    lay_ref,
    in_s,
    tokv,
    wsend,
    wx,
    wst,
    tbl,
    u_ref,
    uown,
    utail,
    utails,
    ucat,
    ut,
    wnat,
    sown,
    scat,
    zsend,
    zown,
    near,
    third,
    fourth,
    far,
    sg,
    sgl,
    sgo,
    ret,
    grad,
    x1_ref,
    gram_sum,
    gram,
    poly,
    rows_ref,
    fin,
    t_s,
    t_r,
    y_s,
    y_r,
    c_s,
    c_r,
    w_s,
    w_r,
    z_s,
    z_r,
    uc_s,
    uc_r,
    sc_s,
    sc_r,
    sg_s,
    sg_r,
    nr_s,
    nr_r,
    th_s,
    th_r,
    fo_s,
    fo_r,
    fr_s,
    fr_r,
    ag_s,
    ag_r,
    rt_s,
    rt_r,
    fn_s,
    fn_r,
    picked,
    for_sibling,
    from_sibling,
    sib_s,
    sib_r,
):
    dp = lax.axis_index("dp")
    me = lax.axis_index("expert")
    x, z = lax.rem(dp, NX), dp // NX
    y, c = me // 2, lax.rem(me, 2)

    def wrap(v, n):
        return lax.rem(v + 2 * n, n)

    def peer(dx=0, dy=0, dz=0, dc=0):
        core = lax.rem(c + dc, 2)
        return (wrap(z + dz, NZ) * NX + wrap(x + dx, NX), wrap(y + dy, NY) * 2 + core)

    def copy(ref_src, ref_dst, ssem, rsem, device):
        return pltpu.make_async_remote_copy(
            src_ref=ref_src,
            dst_ref=ref_dst,
            send_sem=ssem,
            recv_sem=rsem,
            device_id=device,
            device_id_type=MESH,
        )

    def aligned(v, m):
        return pl.multiple_of(v, m)

    barrier = pltpu.get_barrier_semaphore()
    greeted = [(dp, lax.rem(me + i, NE)) for i in range(1, NE)]
    greeted += [peer(dz=k) for k in (-2, -1, 1, 2)]
    greeted += [peer(dx=k) for k in range(1, NX)]
    for device in greeted:
        pl.semaphore_signal(barrier, inc=1, device_id=device, device_id_type=MESH)

    own_rows = pl.ds(aligned(y * (2 * TOK) + c * TOK, TOK), TOK)
    operands = (
        (tok_hbm, tokv.at[own_rows, :]),
        (w_hbm, w_ref),
        (chosen_hbm, chosen_ref),
        (seat_hbm, seat_ref),
        (lay_hbm, lay_ref),
        (gate_hbm, gate_ref),
        (adj_hbm, adj_ref),
    )
    loads = [pltpu.make_async_copy(a, b, in_s.at[i]) for i, (a, b) in enumerate(operands)]
    for cp in loads:
        cp.start()
    for cp in loads[:4]:
        cp.wait()

    chosen = chosen_ref[...]
    quota = jnp.zeros_like(chosen)
    for e in range(2 * NE):
        quota = jnp.where(chosen == e, quota_ref[e], quota)
    code = jnp.where(seat_ref[...] < quota, chosen * 32 + seat_ref[...], -1)
    tbl[me, 0:TOP, :] = code
    tbl[me, TOP:8, :] = jnp.full((8 - TOP, TOK), -1, jnp.int32)

    def tok_rows(yb, cb, p):
        return pl.ds(aligned(yb * (2 * TOK) + cb * TOK + p * PIECE, PIECE), PIECE)

    def wx_rows(xb):
        return pl.ds(aligned(xb * WPAD, WPAD), WPAD)

    blank = jnp.zeros((WPAD - ROWS, D), BF16)
    for l in range(2):
        wsend[l] = jnp.concatenate([w_ref[:, l, :], blank], axis=0)
    for k in range(NX):
        scat[k * DEPTH + SLOTS_E : (k + 1) * DEPTH, :] = jnp.zeros((DEPTH - SLOTS_E, D), BF16)

    r0 = wrap(x - 2 * c, NX)
    is_owner = r0 < 2
    l_own = lax.rem(r0, 2)

    pl.semaphore_wait(barrier, len(greeted))

    sent = []

    def start(cp):
        cp.start()
        sent.append(cp)

    def drain():
        for cp in sent:
            cp.wait_send()
        sent.clear()

    def y_copy(direction, hop, p):
        step = 1 if direction == UP else -1
        yb = wrap(y - step * (hop - 1), NY)
        view = tokv.at[tok_rows(yb, c, p), :]
        at = (direction, hop - 1, p)
        return copy(view, view, y_s.at[at], y_r.at[at], peer(dy=step))

    def y_arrival(direction, hop, p):
        step = 1 if direction == UP else -1
        yb = wrap(y - step * hop, NY)
        view = tokv.at[tok_rows(yb, c, p), :]
        at = (direction, hop - 1, p)
        return yb, copy(view, view, y_s.at[at], y_r.at[at], peer(dy=step))

    def to_sibling(n, p):
        yb = wrap(y + REL[n], NY)
        view = tokv.at[tok_rows(yb, c, p), :]
        start(copy(view, view, c_s.at[n, p], c_r.at[n, p], peer(dc=1)))

    def y_recv(direction, hop, p):
        _, cp = y_arrival(direction, hop, p)
        cp.wait_recv()
        if hop < 3 or (hop == 3 and p == direction):
            start(y_copy(direction, hop + 1, p))
        step = 1 if direction == UP else -1
        n = REL.index(-step * hop) if hop < 4 else 7
        to_sibling(n, p)

    def to_owner(l, make):
        k = wrap(x - 2 * c - l, NX)

        @pl.when(k != 0)
        def _():
            make(k, ((z * NX + 2 * c + l), me)).start()

    def w_copy(l):
        def make(k, device):
            return copy(wsend.at[l], wx.at[wx_rows(x), :], w_s.at[l], w_r.at[k], device)

        return make

    def x_weights():
        for l in range(2):
            to_owner(l, w_copy(l))

    def x_weights_recv():
        wx[wx_rows(x), :] = wsend[l_own]
        for k in range(1, NX):
            view = wx.at[wx_rows(wrap(x + k, NX)), :]
            copy(view, view, w_s.at[0], w_r.at[k], peer(dx=k)).wait_recv()
        pick = jnp.where(
            lax.broadcasted_iota(jnp.int32, (ZBLK, NX * WPAD), 0) == lay_ref[2:3, 0 : NX * WPAD],
            1.0,
            0.0,
        ).astype(BF16)
        wst[pl.ds(aligned(z * ZBLK, 16), ZBLK), :] = dot(pick, wx[...]).astype(BF16)
        for p in range(2):
            for direction in (UP, DOWN):
                z_copy(direction, 1, p).start()

    def z_view(zb, p):
        first, count = ZPIECES[p]
        return wst.at[pl.ds(aligned(zb * ZBLK + first, 16), count), :]

    def z_copy(direction, hop, p):
        step = 1 if direction == UP else -1
        view = z_view(wrap(z - step * (hop - 1), NZ), p)
        at = (direction, hop - 1, p)
        return copy(view, view, z_s.at[at], z_r.at[at], peer(dz=step))

    def z_recv(direction, hop, p):
        step = 1 if direction == UP else -1
        view = z_view(wrap(z - step * hop, NZ), p)
        at = (direction, hop - 1, p)
        copy(view, view, z_s.at[at], z_r.at[at], peer(dz=step)).wait_recv()
        if hop < 3 or (hop == 3 and p == direction):
            z_copy(direction, hop + 1, p).start()

    def z_both(hop, p):
        z_recv(UP, hop, p)
        z_recv(DOWN, hop, p)

    def up_grad(t):
        def tile(i, carry):
            rows = pl.ds(aligned(t * HALF + i * 32, 32), 32)
            g = gate_ref[rows, :].astype(F32)
            a = adj_ref[rows, :].astype(F32)
            u_ref[rows, :] = (a * (g / (1.0 + jnp.exp(-g)))).astype(BF16)
            return carry

        lax.fori_loop(0, HALF // 32, tile, 0)

    def u_copy(l, t):
        rows = pl.ds(t * HALF, HALF)

        def make(k, device):
            return copy(
                uown.at[l, rows, pl.ds(0, 256)],
                ucat.at[rows, pl.ds(aligned(k * DEPTH, DEPTH), 256)],
                uc_s.at[l, t],
                uc_r.at[k, t],
                device,
            )

        return make

    def u_tail_copy(l):
        def make(k, device):
            return copy(utail.at[l], utails.at[k], uc_s.at[l, 2], uc_r.at[k, 2], device)

        return make

    def unpack(k):
        lane = lax.broadcasted_iota(jnp.int32, (HALF, 128), 1)
        both = utails[k].astype(F32)
        for t in range(2):
            moved = both if t == 0 else jnp.concatenate([both[:, 64:], both[:, :64]], axis=1)
            ucat[t * HALF : (t + 1) * HALF, k * DEPTH + 256 : (k + 1) * DEPTH] = jnp.where(
                lane < 64, moved, 0.0
            ).astype(BF16)

    def s_copy(l, g):
        first, count = S_PARTS[g]

        def make(k, device):
            return copy(
                sown.at[l, pl.ds(first, count), :],
                scat.at[pl.ds(aligned(k * DEPTH + first, 16), count), :],
                sc_s.at[l, g],
                sc_r.at[k, g],
                device,
            )

        return make

    def expert_major():
        chip = jnp.bitwise_and(lay_ref[0:1, 0:DEPTH] + y, NY - 1)
        tails = [[], []]
        for t in range(2):
            rows = slice(t * HALF, (t + 1) * HALF)
            up_grad(t)
            for l in range(2):
                source = chip * (4 * CAP) + lay_ref[1:2, 0:DEPTH] + l * CAP
                pick = jnp.where(
                    lax.broadcasted_iota(jnp.int32, (SLOTS, DEPTH), 0) == source, 1.0, 0.0
                ).astype(BF16)
                full = dot(u_ref[rows, :], pick)
                uown[l, rows, :] = full.astype(BF16)
                tails[l].append(full[:, 256 : 256 + 64])
                to_owner(l, u_copy(l, t))
        for l in range(2):
            utail[l] = jnp.concatenate(tails[l], axis=1).astype(BF16)
            to_owner(l, u_tail_copy(l))

    def u_recv():
        ucat[:, 0:DEPTH] = uown[l_own]
        for k in range(1, NX):
            for t in range(2):
                view = ucat.at[pl.ds(t * HALF, HALF), pl.ds(k * DEPTH, 256)]
                copy(view, view, uc_s.at[0, t], uc_r.at[k, t], peer(dx=k)).wait_recv()
            view = utails.at[k]
            copy(view, view, uc_s.at[0, 2], uc_r.at[k, 2], peer(dx=k)).wait_recv()
            unpack(k)

    def transposed(k):
        row = lax.broadcasted_iota(jnp.int32, (SLOTS_E, DEPTH), 0)
        col = lax.broadcasted_iota(jnp.int32, (SLOTS_E, DEPTH), 1)
        same = jnp.where(row == col, 1.0, 0.0).astype(BF16)
        ut[k * SLOTS_E : (k + 1) * SLOTS_E, :] = dot_nt(
            same, ucat[:, k * DEPTH : (k + 1) * DEPTH]
        ).astype(BF16)

    def slot_grads():
        for zb in range(NZ):
            wnat[zb * ZROWS : (zb + 1) * ZROWS, :] = wst[zb * ZBLK : zb * ZBLK + ZROWS, :]
        for n in range(4):
            cols = slice(n * 256, (n + 1) * 256)
            sg[:, cols] = dot(ut[...], wnat[:, cols]).astype(BF16)

    def sg_copy(k, g):
        return copy(
            sg.at[pl.ds(k * SLOTS_E + g * GROUP, GROUP), :],
            sgl.at[l_own, pl.ds(g * GROUP, GROUP), :],
            sg_s.at[k, g],
            sg_r.at[l_own, g],
            peer(dx=k),
        )

    def gather_chip(n):
        yb = wrap(y + REL[n], NY)
        for p in range(2):
            view = tokv.at[tok_rows(yb, 1 - c, p), :]
            copy(view, view, c_s.at[n, p], c_r.at[n, p], peer(dc=1)).wait_recv()
        far = 1 << 12
        codes = jnp.concatenate([tbl[yb * 2], tbl[yb * 2 + 1] + far], axis=1)
        row = lax.broadcasted_iota(jnp.int32, (GROUP, 2 * TOK), 0)
        want = row
        for b in range(1, 4):
            want = jnp.where(row >= b * CAP, row + (b % 2) * far + (b // 2) * 32 - b * CAP, want)
        want = want + (2 * me) * 32
        hit = jnp.zeros((GROUP, 2 * TOK), F32)
        for k in range(TOP):
            hit = hit + jnp.where(codes[k : k + 1, :] == want, 1.0, 0.0)
        tokens = tokv[pl.ds(aligned(yb * 2 * TOK, 2 * TOK), 2 * TOK), :]
        return dot(hit.astype(BF16), tokens)

    def place(g, values):
        first, count = S_PARTS[g]
        rows = slice(first, first + count)
        for l in range(2):
            sown[l, rows, :] = values[l].astype(BF16)
            to_owner(l, s_copy(l, g))

        @pl.when(is_owner)
        def _():
            scat[rows, :] = sown[l_own, rows, :]

    def gather(g):
        two = [gather_chip(n) for n in (2 * g, 2 * g + 1)]
        per = 2 * CAP
        place(g, [jnp.concatenate([v[l * per : (l + 1) * per] for v in two]) for l in range(2)])

    for p in range(2):
        for direction in (UP, DOWN):
            start(y_copy(direction, 1, p))
    x_weights()
    for i in range(1, NE):
        j = lax.rem(me + i, NE)
        start(copy(tbl.at[me], tbl.at[me], t_s.at[i], t_r.at[i], (dp, j)))
    for p in range(2):
        to_sibling(0, p)

    def y_both(hop, p):
        y_recv(UP, hop, p)
        y_recv(DOWN, hop, p)

    for cp in loads[4:]:
        cp.wait()
    expert_major()
    y_both(1, 0)

    @pl.when(is_owner)
    def _():
        x_weights_recv()

    y_both(1, 1)
    for i in range(1, NE):
        j = lax.rem(me + NE - i, NE)
        copy(tbl.at[j], tbl.at[j], t_s.at[i], t_r.at[i], (dp, j)).wait_recv()
    gather(0)

    @pl.when(is_owner)
    def _():
        z_both(1, 0)
        z_both(1, 1)

    y_both(2, 0)

    @pl.when(is_owner)
    def _():
        z_both(2, 0)
        z_both(2, 1)

    y_both(2, 1)
    gather(1)

    @pl.when(is_owner)
    def _():
        z_both(3, 0)
        z_both(3, 1)

    y_both(3, 0)

    @pl.when(is_owner)
    def _():
        u_recv()
        transposed(0)
        transposed(1)

    y_both(3, 1)
    gather(2)
    sixth = gather_chip(6)
    place(3, [sixth[0:32], sixth[40:72]])

    @pl.when(is_owner)
    def _():
        transposed(2)
        transposed(3)
        z_recv(UP, 4, 0)
        z_recv(DOWN, 4, 1)

    y_recv(UP, 4, 0)
    y_recv(DOWN, 4, 1)
    seventh = gather_chip(7)
    place(4, [jnp.concatenate([sixth[32:40], seventh[0:40]]), jnp.concatenate([sixth[72:80], seventh[40:80]])])

    @pl.when(is_owner)
    def _():
        slot_grads()
        for g in (3, 2, 1, 0):
            for k in range(1, NX):
                sg_copy(k, g).start()
        sgl[l_own] = sg[0:SLOTS_E, :]

    z2 = z // 2
    odd = lax.rem(z, 2)
    order = [wrap(z2 + k, 4) for k in (2, 1 + 2 * odd, 3 - 2 * odd, 0)]

    def cols2(i):
        return pl.ds(aligned(order[i] * 256, 256), 256)

    def zchunk(r):
        return pl.ds(aligned(wrap(z + r, NZ) * 128, 128), 128)

    def direct_copy(d):
        r, step = ((1, 1), (7, -1))[d]
        return copy(zsend.at[:, zchunk(r)], near.at[d], nr_s.at[d], nr_r.at[d], peer(dz=step))

    def third_copy(d):
        r, step = ((3, 1), (5, -1))[d]
        return copy(zsend.at[:, zchunk(r)], third.at[d], th_s.at[d], th_r.at[d], peer(dz=step))

    def fourth_copy(d):
        step = (2, -2)[d]
        rows = pl.ds(d * HALF, HALF)
        return copy(
            zsend.at[rows, zchunk(4)], fourth.at[d], fo_s.at[d], fo_r.at[d], peer(dz=step)
        )

    def relayed_copy(d):
        r, step = ((2, 2), (6, -2))[d]
        return copy(zsend.at[:, zchunk(r)], far.at[d], fr_s.at[d], fr_r.at[d], peer(dz=step))

    def relay(d):
        r = (2, 6)[d]
        third_copy(d).wait_recv()
        fourth_copy(d).wait_recv()
        for t in range(2):
            rows = slice(t * HALF, (t + 1) * HALF)
            total = zsend[rows, zchunk(r)].astype(F32) + third[d, rows, :].astype(F32)
            if t == d:
                total = total + fourth[d].astype(F32)
            zsend[rows, zchunk(r)] = total.astype(BF16)
        relayed_copy(d).start()

    @pl.when(is_owner)
    def _():
        for g in range(5):
            for k in range(1, NX):
                view = scat.at[pl.ds(k * DEPTH + S_PARTS[g][0], S_PARTS[g][1]), :]
                copy(view, view, sc_s.at[0, 0], sc_r.at[k, g], peer(dx=k)).wait_recv()
        for i in range(4):
            halves = []
            for t in range(2):
                rows = slice(t * HALF, (t + 1) * HALF)
                halves.append(dot(ucat[rows, :], scat[:, cols2(i)]))
                zsend[rows, cols2(i)] = halves[t].astype(BF16)
            for parity in range(2):

                @pl.when(odd == parity)
                def _():
                    if i == 0:
                        fourth_copy(0).start()
                        fourth_copy(1).start()
                        third_copy(1 - parity).start()
                    elif i == 1:
                        third_copy(parity).start()
                    elif i == 2:
                        direct_copy(1 - parity).start()
                    else:
                        direct_copy(parity).start()
                        first = parity * 128
                        for t in range(2):
                            rows = slice(t * HALF, (t + 1) * HALF)
                            zown[rows, :] = halves[t][:, first : first + 128]

    def chip_rows(yb):
        return pl.ds(aligned(yb * GROUP, 16), GROUP)

    def return_copy(n):
        yb = wrap(y + REL[n], NY)
        return copy(
            sgo.at[pl.ds(n * GROUP, GROUP), :],
            ret.at[chip_rows(y), :],
            rt_s.at[n],
            rt_r.at[n],
            (dp, yb * 2 + c),
        )

    def send_back(g):
        for l in range(2):

            @pl.when(x != 2 * c + l)
            def _():
                view = sgl.at[l, pl.ds(g * GROUP, GROUP), :]
                copy(view, view, sg_s.at[1, g], sg_r.at[l, g], peer(dx=1)).wait_recv()

        for n in (2 * g + 1, 2 * g):
            both = [sgl[l, n * 2 * CAP : (n + 1) * 2 * CAP, :] for l in range(2)]
            sgo[n * GROUP : (n + 1) * GROUP, :] = jnp.concatenate(both, axis=0)
            if n:
                start(return_copy(n))


    drain()
    for l in range(2):
        k = wrap(x - 2 * c - l, NX)

        @pl.when(k != 0)
        def _():
            device = (z * NX + 2 * c + l, me)
            w_copy(l)(k, device).wait_send()
            u_copy(l, 0)(k, device).wait_send()
            u_copy(l, 1)(k, device).wait_send()
            u_tail_copy(l)(k, device).wait_send()
            for g in range(5):
                s_copy(l, g)(k, device).wait_send()

    send_back(3)
    send_back(2)

    @pl.when(is_owner)
    def _():
        relay(0)
        relay(1)

    @pl.when(is_owner)
    def _():
        for hop in range(1, 5):
            for p in range(2):
                for direction in (UP, DOWN):
                    if hop < 4 or p == direction:
                        z_copy(direction, hop, p).wait_send()

    send_back(1)
    send_back(0)
    ret[chip_rows(y), :] = sgo[0:GROUP, :]

    codes = jnp.concatenate([tbl[2 * y], tbl[2 * y + 1] + (1 << 12)], axis=1)
    row = lax.broadcasted_iota(jnp.int32, (GROUP, 2 * TOK), 0)
    want = row
    for b in range(1, 4):
        want = jnp.where(row >= b * CAP, row + (b % 2) * (1 << 12) + (b // 2) * 32 - b * CAP, want)
    picks = []
    for yb in range(NY):
        base = want + (yb * 4 + 2 * c) * 32
        hit = jnp.zeros((GROUP, 2 * TOK), F32)
        for k in range(TOP):
            hit = hit + jnp.where(codes[k : k + 1, :] == base, 1.0, 0.0)
        picks.append(hit)
    picked[...] = jnp.concatenate(picks, axis=0).T.astype(BF16)

    zcols = pl.ds(aligned(z * 128, 128), 128)

    def ag_view(zb, p):
        return grad.at[pl.ds(p * PART, PART), pl.ds(aligned(zb * 128, 128), 128)]

    def ag_copy(direction, hop, p):
        step = 1 if direction == UP else -1
        view = ag_view(wrap(z - step * (hop - 1), NZ), p)
        at = (direction, hop - 1, p)
        return copy(view, view, ag_s.at[at], ag_r.at[at], peer(dz=step))

    def ag_recv(direction, hop, p):
        step = 1 if direction == UP else -1
        view = ag_view(wrap(z - step * hop, NZ), p)
        at = (direction, hop - 1, p)
        copy(view, view, ag_s.at[at], ag_r.at[at], peer(dz=step)).wait_recv()
        if hop < 3 or (hop == 3 and p // 2 == direction):
            ag_copy(direction, hop + 1, p).start()

    def rows_copy(k):
        xd = wrap(x + k, NX)
        return copy(
            rows_ref.at[pl.ds(aligned(xd * 32, 32), 32), :],
            fin.at[l_own],
            fn_s.at[k],
            fn_r.at[l_own],
            peer(dx=k),
        )

    @pl.when(is_owner)
    def _():
        total = zown[...]
        for d in range(2):
            direct_copy(d).wait_recv()
            total = total + near[d].astype(F32)
        for d in range(2):
            relayed_copy(d).wait_recv()
            total = total + far[d].astype(F32)
        grad[:, zcols] = total.astype(BF16)
        for p in range(4):
            for direction in (UP, DOWN):
                ag_copy(direction, 1, p).start()
        squares = jnp.zeros((1, 256), F32)
        for hop in range(1, 5):
            if hop < 4:
                for p in range(4):
                    for direction in (UP, DOWN):
                        ag_recv(direction, hop, p)
                pair = (z - hop, z + hop)
            else:
                for p in range(2):
                    ag_recv(UP, 4, p)
                    ag_recv(DOWN, 4, 2 + p)
                pair = (z + 4, z)
            both = jnp.concatenate(
                [grad[:, pl.ds(aligned(wrap(zb, NZ) * 128, 128), 128)] for zb in pair], axis=1
            )
            wide = both.astype(F32)
            squares = squares + jnp.sum(wide * wide, axis=0, keepdims=True)
            for t in range(2):
                rows = slice(t * HALF, (t + 1) * HALF)
                term = dot_nt(both[rows, :], both)
                if hop > 1:
                    term = gram_sum[rows, :] + term
                if hop < 4:
                    gram_sum[rows, :] = term
                else:
                    norm = jnp.sqrt(jnp.sum(squares, axis=1, keepdims=True))
                    inverse = 1.0 / (norm + EPSILON)
                    gram[rows, :] = (term * inverse * inverse).astype(BF16)

        halves = [slice(0, HALF), slice(HALF, FF)]
        for rows in halves:
            square = dot(gram[rows, :], gram[...])
            poly[rows, :] = (QUINT_B * gram[rows, :].astype(F32) + QUINT_C * square).astype(BF16)
        for rows in halves:
            x1_ref[rows, :] = (
                inverse * (QUINT_A * grad[rows, :].astype(F32) + dot(poly[rows, :], grad[...]))
            ).astype(BF16)
        for rows in halves:
            gram[rows, :] = dot_nt(x1_ref[rows, :], x1_ref[...]).astype(BF16)
        picks = []
        for xd in range(NX):
            r = lax.broadcasted_iota(jnp.int32, (32, FF), 0)
            f = lax.broadcasted_iota(jnp.int32, (32, FF), 1)
            hit = jnp.logical_and(r < ROWS, f == r + (z * NX + xd) * ROWS)
            picks.append(jnp.where(hit, 1.0, 0.0))
        pick = jnp.concatenate(picks, axis=0).astype(BF16)
        gram_rows = dot(pick, gram[...]).astype(BF16)
        it_rows = dot(pick, x1_ref[...])
        poly_rows = (QUINT_B * gram_rows.astype(F32) + QUINT_C * dot(gram_rows, gram[...])).astype(
            BF16
        )
        rows_ref[...] = (QUINT_A * it_rows + dot(poly_rows, x1_ref[...])).astype(BF16)
        for k in range(1, NX):
            rows_copy(k).start()
        fin[l_own] = rows_ref[pl.ds(aligned(x * 32, 32), 32), :]

    for n in range(1, NY):
        view = ret.at[chip_rows(wrap(y - REL[n], NY)), :]
        copy(view, view, rt_s.at[n], rt_r.at[n], peer(dy=-REL[n])).wait_recv()

    def core_rows(core):
        return pl.ds(aligned(core * TOK, TOK), TOK)

    left, right = slice(0, D // 2), slice(D // 2, D)
    sibling = []
    for h, cols in enumerate((left, right)):
        for_sibling[:, cols] = dot(picked[core_rows(1 - c), :], ret[:, cols])
        view = pl.ds(h * (D // 2), D // 2)
        cp = copy(
            for_sibling.at[:, view], from_sibling.at[:, view], sib_s.at[h], sib_r.at[h], peer(dc=1)
        )
        start(cp)
        sibling.append(cp)
    mine = [dot(picked[core_rows(c), :], ret[:, cols]) for cols in (left, right)]

    @pl.when(is_owner)
    def _():
        for d in range(2):
            direct_copy(d).wait_send()
            third_copy(d).wait_send()
            fourth_copy(d).wait_send()
            relayed_copy(d).wait_send()
        for hop in range(1, 5):
            for p in range(4):
                for direction in (UP, DOWN):
                    if hop < 4 or p // 2 == direction:
                        ag_copy(direction, hop, p).wait_send()
        for g in range(4):
            for k in range(1, NX):
                sg_copy(k, g).wait_send()

    for h, cols in enumerate((left, right)):
        sibling[h].wait_recv()
        out_tok[:, cols] = (mine[h] + from_sibling[:, cols]).astype(BF16)

    for l in range(2):
        owner_x = 2 * c + l

        @pl.when(x != owner_x)
        def _():
            view = fin.at[l]
            copy(view, view, fn_s.at[1], fn_r.at[l], peer(dx=1)).wait_recv()

        out_rows[l] = fin[l]

    drain()

    @pl.when(is_owner)
    def _():
        for k in range(1, NX):
            rows_copy(k).wait_send()


def results(token_ref, rows_ref, out_tok, out_mu):
    scale = 0.2 * math.sqrt(max(FF, D))
    out_tok[...] = token_ref[...]
    for l in range(2):
        out_mu[:, l, :] = scale * rows_ref[l, 0:ROWS, :].astype(F32)


def body(tokens, weights, gate, adjoint, chosen, seat, quota):
    vmem = pl.BlockSpec(memory_space=pltpu.VMEM)
    anywhere = pl.BlockSpec(memory_space=pl.ANY)
    sem = pltpu.SemaphoreType.DMA
    scratch = [
        pltpu.VMEM((ROWS, 2, D), BF16),
        pltpu.VMEM((FF, SLOTS), BF16),
        pltpu.VMEM((FF, SLOTS), BF16),
        pltpu.VMEM((TOP, TOK), jnp.int32),
        pltpu.VMEM((TOP, TOK), jnp.int32),
        pltpu.VMEM((8, DEPTH), jnp.int32),
        sem((7,)),
        pltpu.VMEM((NE * TOK, D), BF16),
        pltpu.VMEM((2, WPAD, D), BF16),
        pltpu.VMEM((NX * WPAD, D), BF16),
        pltpu.VMEM((NZ * ZBLK, D), BF16),
        pltpu.VMEM((NE, 8, TOK), jnp.int32),
        pltpu.VMEM((FF, SLOTS), BF16),
        pltpu.VMEM((2, FF, DEPTH), BF16),
        pltpu.VMEM((2, HALF, 128), BF16),
        pltpu.VMEM((NX, HALF, 128), BF16),
        pltpu.VMEM((FF, NX * DEPTH), BF16),
        pltpu.VMEM((NX * SLOTS_E, FF), BF16),
        pltpu.VMEM((FF, D), BF16),
        pltpu.VMEM((2, SLOTS_E, D), BF16),
        pltpu.VMEM((NX * DEPTH, D), BF16),
        pltpu.VMEM((FF, D), BF16),
        pltpu.VMEM((FF, 128), F32),
        pltpu.VMEM((2, FF, 128), BF16),
        pltpu.VMEM((2, FF, 128), BF16),
        pltpu.VMEM((2, HALF, 128), BF16),
        pltpu.VMEM((2, FF, 128), BF16),
        pltpu.VMEM((NX * SLOTS_E, D), BF16),
        pltpu.VMEM((2, SLOTS_E, D), BF16),
        pltpu.VMEM((SLOTS, D), BF16),
        pltpu.VMEM((SLOTS, D), BF16),
        pltpu.VMEM((FF, D), BF16),
        pltpu.VMEM((FF, D), BF16),
        pltpu.VMEM((FF, FF), F32),
        pltpu.VMEM((FF, FF), BF16),
        pltpu.VMEM((FF, FF), BF16),
        pltpu.VMEM((128, D), BF16),
        pltpu.VMEM((2, 32, D), BF16),
        sem((NE,)),
        sem((NE,)),
        sem((2, 4, 2)),
        sem((2, 4, 2)),
        sem((8, 2)),
        sem((8, 2)),
        sem((2,)),
        sem((NX,)),
        sem((2, 4, 2)),
        sem((2, 4, 2)),
        sem((2, 3)),
        sem((NX, 3)),
        sem((2, 5)),
        sem((NX, 5)),
        sem((NX, 4)),
        sem((2, 4)),
        sem((2,)),
        sem((2,)),
        sem((2,)),
        sem((2,)),
        sem((2,)),
        sem((2,)),
        sem((2,)),
        sem((2,)),
        sem((2, 4, 4)),
        sem((2, 4, 4)),
        sem((NY,)),
        sem((NY,)),
        sem((NX,)),
        sem((2,)),
        pltpu.VMEM((2 * TOK, SLOTS), BF16),
        pltpu.VMEM((TOK, D), F32),
        pltpu.VMEM((TOK, D), F32),
        sem((2,)),
        sem((2,)),
    ]
    token_grad, update_rows = pl.pallas_call(
        kernel,
        out_shape=(
            jax.ShapeDtypeStruct((TOK, D), BF16),
            jax.ShapeDtypeStruct((2, 32, D), BF16),
        ),
        in_specs=[anywhere] * 6 + [pl.BlockSpec(memory_space=pltpu.SMEM), anywhere],
        out_specs=(vmem, vmem),
        scratch_shapes=scratch,
        compiler_params=pltpu.CompilerParams(
            collective_id=0, has_side_effects=True, vmem_limit_bytes=60 * 2**20
        ),
        cost_estimate=pl.CostEstimate(
            flops=16 * 10**9, bytes_accessed=5 * 10**6, transcendentals=450560
        ),
        name="expert_backward",
    )(tokens, weights, gate, adjoint, chosen.T, seat.T, quota, jnp.asarray(layout_tables()))
    return pl.pallas_call(
        results,
        out_shape=(
            jax.ShapeDtypeStruct((TOK, D), BF16),
            jax.ShapeDtypeStruct((ROWS, 2, D), F32),
        ),
        in_specs=[vmem] * 2,
        out_specs=(vmem, vmem),
        cost_estimate=pl.CostEstimate(flops=45056, bytes_accessed=10**6, transcendentals=0),
        name="results",
    )(token_grad, update_rows)


def solution(mesh):
    return jax.shard_map(
        body,
        mesh=mesh,
        in_specs=(
            P(("dp", "expert"), None),
            P("dp", "expert", None),
            P(None, ("dp", "expert")),
            P(None, ("dp", "expert")),
            P(("dp", "expert"), None),
            P(("dp", "expert"), None),
            P(),
        ),
        out_specs=(P(("dp", "expert"), None), P("dp", "expert", None)),
        check_vma=False,
    )
```
